256 devices in a mesh: img: 128 (over z, x_lo, y, core), tok: 2 (over x_hi).
Axes of the slice: x: 4 (x_hi: 2, x_lo: 2; x = x_hi * 2 + x_lo), y: 4, z: 8, core: 2. Of those that a mesh axis runs over, the one named last changes fastest.
Arguments:
- tokens: bfloat16 [128, 256, 1280], P('img', 'tok'), may hold values from -6 to 6
- grad_out: bfloat16 [128, 256, 1280], P('img', 'tok'), may hold values from -6 to 6
- router: bfloat16 [1280, 64], replicated, may hold values from -0.15625 to 0.15625
- slot_scale: float32 [64], replicated, may hold values from 1 to 8
- w_in: bfloat16 [128, 1280, 2048], P('img', None, 'tok'), may hold values from -0.15625 to 0.15625
- w_out: bfloat16 [128, 2048, 1280], P('img', 'tok'), may hold values from -0.09375 to 0.09375
Outputs:
- combined: bfloat16 [128, 256, 1280], P('img', 'tok')
- grad_tokens: bfloat16 [128, 256, 1280], P('img', 'tok')
- grad_router: float32 [1280, 64], replicated
- grad_scale: float32 [64], replicated
- grad_w_in: bfloat16 [128, 1280, 2048], P('img', None, 'tok')
- grad_w_out: bfloat16 [128, 2048, 1280], P('img', 'tok')
The draws below stay inside these ranges and needn't reach their ends.
All inputs are finite; a program needn't handle non-finite values.
Results may differ from the reference program's by a relative error of at most 0.015.
Values may be sent and summed in bfloat16 or wider, within the bound.
A program may use at most 64 MiB of HBM per device.

```python
import math
import jax
import jax.numpy as jnp
from jax import lax

D = 1280
FF = 4096
TOKENS = 256
EXPERTS = 64
IMAGES = 128


def levels(stream_key, extent, pieces, least, largest):
    loudness, own = 1.0, jax.random.fold_in(stream_key, 6)
    for position, shards_of in pieces:
        heights = jnp.exp(jax.random.uniform(jax.random.fold_in(own, position), (shards_of,), jnp.float32, least / len(pieces), largest / len(pieces)))
        loudness = loudness * jnp.repeat(heights, extent[position] // shards_of).reshape([-1 if axis == position else 1 for axis in range(len(extent))])
    return loudness


def centred(own_key, shape, width, bound, shards=(), dtype=jnp.bfloat16):
    factor_of = levels(own_key, shape, shards, -0.22, 0.18) if shards else 1.0
    array = jax.random.normal(own_key, shape, jnp.float32) * width * factor_of
    return jnp.minimum(jnp.maximum(array, -bound), bound).astype(dtype)


def setup_inputs(seed: int = 0) -> dict:
    streams_of = jax.random.split(jax.random.key(seed), 7)
    return {
        "tokens": centred(streams_of[0], (IMAGES, TOKENS, D), 1.0, 6.0, ((0, 128), (1, 2))),
        "grad_out": centred(streams_of[1], (IMAGES, TOKENS, D), 1.0, 6.0, ((0, 128), (1, 2))),
        "router": centred(streams_of[2], (D, EXPERTS), D ** -0.5, 0.15625),
        "slot_scale": jnp.clip(jnp.exp(jax.random.uniform(streams_of[3], (EXPERTS,), jnp.float32, math.log(1.0), math.log(8.0))), 1.0, 8.0),
        "w_in": centred(streams_of[4], (2 * EXPERTS, D, FF // 2), D ** -0.5, 0.15625, ((0, 128), (2, 2))),
        "w_out": centred(streams_of[5], (2 * EXPERTS, FF // 2, D), FF ** -0.5, 0.09375, ((0, 128), (1, 2))),
    }


EPSILON = 1e-06
ROOT_HALF = 0.7071067811865476
DENSITY = 0.3989422804014327

def gelu_value(values):
    return values * (0.5 * (1.0 + lax.erf(values * ROOT_HALF)))

def gelu_slope(values):
    return 0.5 * (1.0 + lax.erf(values * ROOT_HALF)) + values * jnp.exp(-0.5 * values * values) * DENSITY

def reference(tokens, grad_out, router, slot_scale, w_in, w_out):
    single = jnp.float32
    half_type = jnp.bfloat16
    router_f = router.astype(single)
    inv_p = lax.rsqrt(lax.optimization_barrier(jnp.sum(router_f * router_f, 0)) + EPSILON)
    column = inv_p * slot_scale

    def front(image):
        raw = jnp.dot(image, router, preferred_element_type=single)
        image_f = image.astype(single)
        inv_x = lax.rsqrt(lax.optimization_barrier(jnp.sum(image_f * image_f, 1)) + EPSILON)
        logit = raw * inv_x[:, None] * column[None, :]
        expo = jnp.exp(logit)
        den = lax.optimization_barrier(jnp.sum(expo, 0))
        numer = jnp.dot(expo.astype(half_type).T, image, preferred_element_type=single)
        slots = (numer / den[:, None]).astype(half_type)
        return (slots, logit, den)
    slots, logits, dens = lax.map(front, tokens)
    halves_in = jnp.transpose(w_in.reshape(2, EXPERTS, D, FF // 2), (1, 0, 2, 3))
    halves_out = jnp.transpose(w_out.reshape(2, EXPERTS, FF // 2, D), (1, 0, 2, 3))
    rows = jnp.transpose(slots, (1, 0, 2))

    def expert_fwd(items):
        rows_e, first_w, second_w = items
        total = jnp.zeros((IMAGES, D), single)
        for copy in range(2):
            act = jnp.dot(rows_e, first_w[copy], preferred_element_type=single)
            hidden = gelu_value(act).astype(half_type)
            part = jnp.dot(hidden, second_w[copy], preferred_element_type=single).astype(half_type)
            total = total + part.astype(single)
        return total.astype(half_type)
    ys = jnp.transpose(lax.map(expert_fwd, (rows, halves_in, halves_out)), (1, 0, 2))

    def middle(items):
        logit, ys_image, grad_image = items
        expo = jnp.exp(logit)
        comb = expo / lax.optimization_barrier(jnp.sum(expo, 1, keepdims=True))
        comb_b = comb.astype(half_type)
        output = jnp.dot(comb_b, ys_image, preferred_element_type=single).astype(half_type)
        dys = jnp.dot(comb_b.T, grad_image, preferred_element_type=single).astype(half_type)
        dcomb = jnp.dot(grad_image, ys_image.T, preferred_element_type=single)
        dlc = comb * (dcomb - lax.optimization_barrier(jnp.sum(comb * dcomb, 1, keepdims=True)))
        return (output, dys, dlc)
    combined, dys, dlcs = lax.map(middle, (logits, ys, grad_out))
    dz_all = jnp.transpose(dys, (1, 0, 2))

    def expert_bwd(items):
        rows_e, dz_e, first_w, second_w = items
        total = jnp.zeros((IMAGES, D), single)
        first_list = []
        second_list = []
        for copy in range(2):
            act = jnp.dot(rows_e, first_w[copy], preferred_element_type=single)
            hidden = gelu_value(act).astype(half_type)
            grad_h = jnp.dot(dz_e, second_w[copy].T, preferred_element_type=single)
            dact = (grad_h * gelu_slope(act)).astype(half_type)
            part = jnp.dot(dact, first_w[copy].T, preferred_element_type=single).astype(half_type)
            total = total + part.astype(single)
            first_list.append(jnp.dot(rows_e.T, dact, preferred_element_type=single).astype(half_type))
            second_list.append(jnp.dot(hidden.T, dz_e, preferred_element_type=single).astype(half_type))
        return (total.astype(half_type), jnp.stack(first_list), jnp.stack(second_list))
    drows, first_grads, second_grads = lax.map(expert_bwd, (rows, dz_all, halves_in, halves_out))
    dxs = jnp.transpose(drows, (1, 0, 2))

    def router_bwd(carry, items):
        outer_acc, total_acc = carry
        image, logit, den, dxs_image, dlc = items
        image_f = image.astype(single)
        inv_x = lax.rsqrt(lax.optimization_barrier(jnp.sum(image_f * image_f, 1)) + EPSILON)
        expo = jnp.exp(logit)
        disp_w = expo / den[None, :]
        weights_b = expo.astype(half_type)
        ddisp = jnp.dot(image, dxs_image.T, preferred_element_type=single)
        corr = lax.optimization_barrier(jnp.sum(disp_w * ddisp, 0))
        grad_l = disp_w * (ddisp - corr[None, :]) + dlc
        product = grad_l * logit
        signal = lax.optimization_barrier(jnp.sum(product, 1))
        grad_q = (grad_l * column[None, :] * inv_x[:, None]).astype(half_type)
        scaled = (dxs_image.astype(single) / den[:, None]).astype(half_type)
        grad_image = jnp.dot(weights_b, scaled, preferred_element_type=single)
        grad_image = grad_image + jnp.dot(grad_q, router.T, preferred_element_type=single)
        grad_image = grad_image - (inv_x * inv_x * signal)[:, None] * image_f
        outer_acc = outer_acc + jnp.dot(image.T, grad_q, preferred_element_type=single)
        total_acc = total_acc + lax.optimization_barrier(jnp.sum(product, 0))
        return ((outer_acc, total_acc), grad_image.astype(half_type))
    start = (jnp.zeros((D, EXPERTS), single), jnp.zeros((EXPERTS,), single))
    (outer, total), grad_tokens = lax.scan(router_bwd, start, (tokens, logits, dens, dxs, dlcs))
    grad_router = outer - (inv_p * inv_p * total)[None, :] * router_f
    grad_scale = total / slot_scale
    grad_w_in = jnp.transpose(first_grads, (1, 0, 2, 3)).reshape(2 * EXPERTS, D, FF // 2)
    grad_w_out = jnp.transpose(second_grads, (1, 0, 2, 3)).reshape(2 * EXPERTS, FF // 2, D)
    return (combined, grad_tokens, grad_router, grad_scale, grad_w_in, grad_w_out)
```

```python
import jax
import jax.numpy as jnp
from jax import lax
from jax.experimental import pallas as pl
from jax.experimental.pallas import tpu as pltpu
from jax.sharding import PartitionSpec as P

EPSILON = 1e-06
ROOT_HALF = 0.7071067811865476
DENSITY = 0.3989422804014327
MESH = pl.DeviceIdType.MESH
F32 = jnp.float32
BF16 = jnp.bfloat16
D = 1280
HALF = 640
E = 64
M = 128
H = 1024


def mm(a, b):
    return lax.dot_general(a, b, (((1,), (0,)), ((), ())), preferred_element_type=F32)


def mm_nt(a, b):
    return lax.dot_general(a, b, (((1,), (1,)), ((), ())), preferred_element_type=F32)


def mm_tn(a, b):
    return lax.dot_general(a, b, (((0,), (0,)), ((), ())), preferred_element_type=F32)


def pick(rows, cols):
    n = rows.shape[0]
    at = lax.broadcasted_iota(jnp.int32, (n, cols), 1)
    return jnp.where(at == rows, 1.0, 0.0).astype(BF16)


def to_row(col):
    n = col.shape[0]
    same = lax.broadcasted_iota(jnp.int32, (n, n), 0) == lax.broadcasted_iota(jnp.int32, (n, n), 1)
    return jnp.sum(jnp.where(same, col, 0.0), 0, keepdims=True)


def to_col(row):
    n = row.shape[1]
    same = lax.broadcasted_iota(jnp.int32, (n, n), 0) == lax.broadcasted_iota(jnp.int32, (n, n), 1)
    return jnp.sum(jnp.where(same, row, 0.0), 1, keepdims=True)


def layer(
    tokens_h, gout_h, w1_h, w2_h, router_ref, scale_ref,
    combined_ref, gtok_ref, x_ref, z_ref, hid_ref, dact_ref, groute_ref, gscale_ref,
    tok, gout, w1, w2, pack_m, unpack_m,
    part_tx, part_rx, den_tx, den_rx, own_a, sib_a, msg_tx, msg_rx, swap_tx, swap_rx,
    slope, own_b, swap2_tx, swap2_rx, msg2_tx, msg2_rx, swap3_tx, swap3_rx, sum_tx, sum_rx,
    ar_tx, ar_rx1, ar_rx2, ar_rx3, ar_rx4,
    load_sem, pair_ss, pair_rs, a2a_ss, a2a_rs, ar_ss, ar_rs,
):
    img = lax.axis_index("img")
    t = lax.axis_index("tok")
    half = img // 64
    core = lax.rem(img, 2)
    idx = lax.rem(img, 64) // 2
    sib = {"img": img + 1 - 2 * core, "tok": t}
    partner = {"img": img, "tok": 1 - t}

    def chip(m):
        return {"img": core * 64 + m * 2 + half, "tok": t}

    x_lo = lax.rem(img // 8, 2)
    y = lax.rem(img // 2, 4)
    z = img // 16
    mine = x_lo * 4 + core * 2 + t
    base = img - x_lo * 8 - core

    def near(p):
        return {"img": base + (p // 4) * 8 + lax.rem(p // 2, 2), "tok": lax.rem(p, 2)}

    def along_y(v):
        return {"img": img + (v - y) * 2, "tok": t}

    def along_z(v):
        return {"img": img + (v - z) * 16, "tok": t}

    loads = [
        pltpu.make_async_copy(src, dst, load_sem.at[i])
        for i, (src, dst) in enumerate(((tokens_h, tok), (gout_h, gout), (w1_h, w1), (w2_h, w2)))
    ]
    for load in loads:
        load.start()

    barrier = pltpu.get_barrier_semaphore()
    same = half == core

    def greet(dev):
        pl.semaphore_signal(barrier, inc=1, device_id=dev, device_id_type=MESH)

    greet(sib)
    greet(partner)
    for d in range(1, 8):
        greet(near(lax.rem(mine + d, 8)))
        greet(along_z(lax.rem(z + d, 8)))
    for d in range(1, 4):
        greet(along_y(lax.rem(y + d, 4)))

    def greet_chip(j, c):
        greet(chip(lax.rem(j + idx, 32)))
        return c

    lax.fori_loop(1, 32, greet_chip, 0)

    @pl.when(jnp.logical_not(same))
    def _():
        greet(chip(idx))

    row = lax.broadcasted_iota(jnp.int32, (512, 1), 0)
    m_of = lax.rem(row // 16 + idx, 32)
    side, u, a, v = (row // 8) % 2, (row // 4) % 2, (row // 2) % 2, row % 2
    w = jnp.where(u == core, 0, 1)
    pack_m[...] = pick(side * 256 + w * 128 + a * 64 + 2 * m_of + v, 512)
    w, side, a, m_of, u = row // 256, (row // 128) % 2, (row // 64) % 2, (row // 2) % 32, row % 2
    v = jnp.where(w == 0, core, 1 - core)
    unpack_m[...] = pick(m_of * 16 + side * 8 + u * 4 + a * 2 + v, 512)

    def remote(src, dst, ss, rs, dev):
        return pltpu.make_async_remote_copy(
            src_ref=src, dst_ref=dst, send_sem=ss, recv_sem=rs, device_id=dev, device_id_type=MESH
        )

    eye = pick(lax.broadcasted_iota(jnp.int32, (E, 1), 0), E)
    router_t = mm_nt(eye, router_ref[...])
    router_b = router_t.astype(BF16)
    inv_p = lax.rsqrt(jnp.sum(router_t * router_t, 1, keepdims=True) + EPSILON)
    scale = to_col(scale_ref[...])
    column = inv_p * scale
    loads[0].wait()
    tok_f = tok[...].astype(F32)
    inv_x = to_row(lax.rsqrt(jnp.sum(tok_f * tok_f, 1, keepdims=True) + EPSILON))
    logit = mm_nt(router_b, tok[...]) * inv_x * column
    expo = jnp.exp(logit)
    den_part = jnp.sum(expo, 1, keepdims=True)
    den_tx[...] = jnp.broadcast_to(den_part, (E, 128))
    pw = expo.astype(BF16)
    numer = mm(pw, tok[...])
    part_tx[0:E, :] = numer.astype(BF16)

    count = 1 + 1 + 7 + 7 + 3 + 31 + jnp.where(same, 0, 1)
    pl.semaphore_wait(barrier, count)

    c_den = remote(den_tx, den_rx, pair_ss.at[0], pair_rs.at[0], partner)
    c_den.start()
    c_num = remote(part_tx.at[0:E], part_rx.at[0:E], pair_ss.at[1], pair_rs.at[1], partner)
    c_num.start()
    comb = expo / jnp.sum(expo, 0, keepdims=True)
    comb_b = comb.astype(BF16)
    loads[1].wait()
    dys = mm(comb_b, gout[...])
    part_tx[E:, :] = dys.astype(BF16)
    c_dys = remote(part_tx.at[E:], part_rx.at[E:], pair_ss.at[2], pair_rs.at[2], partner)
    c_dys.start()

    c_den.wait_recv()
    den = den_part + den_rx[...][:, 0:1]
    c_num.wait_recv()
    own_a[0:E, :] = ((numer + part_rx[0:E, :].astype(F32)) / den).astype(BF16)
    c_s1 = remote(own_a.at[0:E], sib_a.at[0:E], pair_ss.at[3], pair_rs.at[3], sib)
    c_s1.start()
    c_dys.wait_recv()
    own_a[E:, :] = (dys + part_rx[E:, :].astype(F32)).astype(BF16)
    c_s2 = remote(own_a.at[E:], sib_a.at[E:], pair_ss.at[4], pair_rs.at[4], sib)
    c_s2.start()
    c_s1.wait_recv()
    c_s2.wait_recv()

    def message(m, tx, rx, way):
        return remote(tx.at[m], rx.at[idx], a2a_ss.at[m], a2a_rs.at[way], chip(lax.rem(m + idx, 32)))

    def spread(own, other, tx, rx, way):
        rows = jnp.concatenate([own[:, :HALF], other[:, :HALF], own[:, HALF:], other[:, HALF:]], 0)

        def chunk(q, c):
            at = pl.ds(pl.multiple_of(q * 128, 128), 128)
            block = mm(pack_m[at, :], rows).astype(BF16).reshape(8, 16, HALF)
            tx[pl.ds(pl.multiple_of(q * 8, 8), 8)] = block

            def send(m, c):
                @pl.when(jnp.logical_or(m > 0, jnp.logical_not(same)))
                def _():
                    message(m, tx, rx, way).start()

                @pl.when(jnp.logical_and(m == 0, same))
                def _():
                    pltpu.make_async_copy(tx.at[0], rx.at[idx], a2a_rs.at[way]).start()

                return c

            lax.fori_loop(q * 8, q * 8 + 8, send, 0)
            return c

        lax.fori_loop(0, 4, chunk, 0)

    def landed(tx, rx, way):
        pltpu.make_async_copy(rx, rx, a2a_rs.at[way]).wait()

        def sent(m, c):
            @pl.when(jnp.logical_or(m > 0, jnp.logical_not(same)))
            def _():
                message(m, tx, rx, way).wait_send()

            return c

        lax.fori_loop(0, 32, sent, 0)

    def gather(w, rx):
        rows = rx[...].reshape(512, HALF)
        left = mm(unpack_m[w * 256:w * 256 + 128, :], rows)
        right = mm(unpack_m[w * 256 + 128:w * 256 + 256, :], rows)
        return left, right

    spread(own_a[...], sib_a[...], msg_tx, msg_rx, 0)
    landed(msg_tx, msg_rx, 0)
    left, right = gather(1, msg_rx)
    swap_tx[:, :HALF] = left.astype(BF16)
    swap_tx[:, HALF:] = right.astype(BF16)
    c_w1 = remote(swap_tx, swap_rx, pair_ss.at[5], pair_rs.at[5], sib)
    c_w1.start()
    left, right = gather(0, msg_rx)
    left, right = left.astype(BF16), right.astype(BF16)
    x_ref[0:64, :HALF] = left[0:64]
    x_ref[0:64, HALF:] = right[0:64]
    z_ref[0:64, :HALF] = left[64:]
    z_ref[0:64, HALF:] = right[64:]
    c_w1.wait_recv()
    x_ref[64:, :] = swap_rx[0:64, :]
    z_ref[64:, :] = swap_rx[64:, :]

    loads[2].wait()
    loads[3].wait()

    def expert_in(n, c):
        at = pl.ds(pl.multiple_of(n * 256, 256), 256)
        act = mm(x_ref[...], w1[:, at])
        phi = 0.5 * (1.0 + lax.erf(act * ROOT_HALF))
        hid_ref[:, at] = (act * phi).astype(BF16)
        slope[:, at] = phi + act * jnp.exp(-0.5 * act * act) * DENSITY
        return c

    lax.fori_loop(0, H // 256, expert_in, 0)

    def expert_out(n, c):
        at = pl.ds(pl.multiple_of(n * 256, 256), 256)
        part = mm(hid_ref[...], w2[:, at]).astype(BF16)
        own_b[0:64, at] = part[0:64]
        swap2_tx[0:64, at] = part[64:]
        return c

    lax.fori_loop(0, D // 256, expert_out, 0)
    c_w2 = remote(swap2_tx.at[0:64], swap2_rx.at[0:64], pair_ss.at[6], pair_rs.at[6], sib)
    c_w2.start()

    def expert_back(n, c):
        at = pl.ds(pl.multiple_of(n * 256, 256), 256)
        dh = mm_nt(z_ref[...], w2[at, :])
        dact_ref[:, at] = (dh * slope[:, at]).astype(BF16)
        return c

    lax.fori_loop(0, H // 256, expert_back, 0)

    def expert_back_in(n, c):
        at = pl.ds(pl.multiple_of(n * 256, 256), 256)
        part = mm_nt(dact_ref[...], w1[at, :]).astype(BF16)
        own_b[64:, at] = part[0:64]
        swap2_tx[64:, at] = part[64:]
        return c

    lax.fori_loop(0, D // 256, expert_back_in, 0)
    c_w3 = remote(swap2_tx.at[64:], swap2_rx.at[64:], pair_ss.at[7], pair_rs.at[7], sib)
    c_w3.start()
    c_w2.wait_recv()
    c_w3.wait_recv()

    spread(own_b[...], swap2_rx[...], msg2_tx, msg2_rx, 1)
    landed(msg2_tx, msg2_rx, 1)
    left, right = gather(1, msg2_rx)
    swap3_tx[:, :HALF] = left.astype(BF16)
    swap3_tx[:, HALF:] = right.astype(BF16)
    c_w4 = remote(swap3_tx, swap3_rx, pair_ss.at[8], pair_rs.at[8], sib)
    c_w4.start()
    left, right = gather(0, msg2_rx)
    c_w4.wait_recv()
    left = left + swap3_rx[:, :HALF].astype(F32)
    right = right + swap3_rx[:, HALF:].astype(F32)
    sum_tx[:, :HALF] = left.astype(BF16)
    sum_tx[:, HALF:] = right.astype(BF16)
    c_sum = remote(sum_tx, sum_rx, pair_ss.at[9], pair_rs.at[9], partner)
    c_sum.start()
    c_sum.wait_recv()
    both = (jnp.concatenate([left, right], 1) + sum_rx[...].astype(F32)).astype(BF16)
    ys, dxs = both[0:64], both[64:]

    dcomb = mm_nt(ys, gout[...])
    dlc = comb * (dcomb - jnp.sum(comb * dcomb, 0, keepdims=True))
    ddisp = mm_nt(dxs, tok[...])
    dxs_f = dxs.astype(F32)
    corr = jnp.sum(own_a[0:E, :].astype(F32) * dxs_f, 1, keepdims=True)
    grad_l = expo / den * (ddisp - corr) + dlc
    grad_q = (grad_l * column * inv_x).astype(BF16)
    outer = mm(grad_q, tok[...])
    for p in range(8):
        ar_tx[p] = outer[16 * (p // 2):16 * (p // 2) + 16, HALF * (p % 2):HALF * (p % 2) + HALF].astype(BF16)
    ar1 = []
    for d in range(1, 8):
        p = lax.rem(mine + d, 8)
        c = remote(ar_tx.at[p], ar_rx1.at[mine], ar_ss.at[d], ar_rs.at[0], near(p))
        c.start()
        ar1.append(c)
    ar_rx1[mine] = ar_tx[mine]

    signal = jnp.sum(grad_l * logit, 0, keepdims=True)
    coef = to_col(inv_x * inv_x * signal)
    scaled = (dxs_f / den).astype(BF16)
    weights = jnp.concatenate([pw, grad_q], 0)
    values = jnp.concatenate([scaled, router_b], 0)
    gtok_ref[...] = (mm_tn(weights, values) - coef * tok_f).astype(BF16)
    combined_ref[...] = mm_tn(comb_b, ys).astype(BF16)

    def all_in(rx, n, stage):
        pltpu.make_async_copy(rx.at[0:n], rx.at[0:n], ar_rs.at[stage]).wait()

    def total_of(rx, n):
        acc = rx[0].astype(F32)
        for j in range(1, n):
            acc = acc + rx[j].astype(F32)
        return acc.astype(BF16)

    all_in(ar_rx1, 7, 0)
    for c in ar1:
        c.wait_send()
    ar_rx2[y] = total_of(ar_rx1, 8)
    ar2 = []
    for d in range(1, 4):
        c = remote(ar_rx2.at[y], ar_rx2.at[y], ar_ss.at[d], ar_rs.at[1], along_y(lax.rem(y + d, 4)))
        c.start()
        ar2.append(c)
    all_in(ar_rx2, 3, 1)
    for c in ar2:
        c.wait_send()
    ar_rx3[z] = total_of(ar_rx2, 4)
    ar3 = []
    for d in range(1, 8):
        c = remote(ar_rx3.at[z], ar_rx3.at[z], ar_ss.at[d], ar_rs.at[2], along_z(lax.rem(z + d, 8)))
        c.start()
        ar3.append(c)
    all_in(ar_rx3, 7, 2)
    for c in ar3:
        c.wait_send()
    ar_rx4[mine] = total_of(ar_rx3, 8)
    ar4 = []
    for d in range(1, 8):
        c = remote(ar_rx4.at[mine], ar_rx4.at[mine], ar_ss.at[d], ar_rs.at[3], near(lax.rem(mine + d, 8)))
        c.start()
        ar4.append(c)
    all_in(ar_rx4, 7, 3)
    for c in ar4:
        c.wait_send()
    whole = jnp.concatenate(
        [jnp.concatenate([ar_rx4[2 * r], ar_rx4[2 * r + 1]], 1) for r in range(4)], 0
    ).astype(F32)
    total = jnp.sum(whole * router_t, 1, keepdims=True)
    groute_ref[...] = whole - inv_p * inv_p * total * router_t
    gscale_ref[...] = jnp.broadcast_to(total / scale, (E, 128))

    for c in (c_den, c_num, c_dys, c_s1, c_s2, c_w1, c_w2, c_w3, c_w4, c_sum):
        c.wait_send()


def shards(tokens, grad_out, router, slot_scale, w_in, w_out):
    any_space = pl.BlockSpec(memory_space=pl.ANY)
    vmem = pl.BlockSpec(memory_space=pltpu.VMEM)
    rows = pltpu.VMEM((128, D), BF16)
    msgs = pltpu.VMEM((32, 16, HALF), BF16)
    dma = pltpu.SemaphoreType.DMA
    out = pl.pallas_call(
        layer,
        out_shape=[
            jax.ShapeDtypeStruct((M, D), BF16),
            jax.ShapeDtypeStruct((M, D), BF16),
            jax.ShapeDtypeStruct((128, D), BF16),
            jax.ShapeDtypeStruct((128, D), BF16),
            jax.ShapeDtypeStruct((128, H), BF16),
            jax.ShapeDtypeStruct((128, H), BF16),
            jax.ShapeDtypeStruct((E, D), F32),
            jax.ShapeDtypeStruct((E, 128), F32),
        ],
        in_specs=[any_space] * 4 + [vmem] * 2,
        out_specs=[vmem] * 8,
        scratch_shapes=[
            rows, rows, pltpu.VMEM((D, H), BF16), pltpu.VMEM((H, D), BF16),
            pltpu.VMEM((512, 512), BF16), pltpu.VMEM((512, 512), BF16),
            rows, rows, pltpu.VMEM((E, 128), F32), pltpu.VMEM((E, 128), F32),
            rows, rows, msgs, msgs, rows, rows,
            pltpu.VMEM((128, H), F32), rows, rows, rows, msgs, msgs, rows, rows, rows, rows,
            pltpu.VMEM((8, 16, HALF), BF16), pltpu.VMEM((8, 16, HALF), BF16),
            pltpu.VMEM((4, 16, HALF), BF16), pltpu.VMEM((8, 16, HALF), BF16),
            pltpu.VMEM((8, 16, HALF), BF16),
            dma((4,)), dma((10,)), dma((10,)), dma((32,)), dma((2,)), dma((8,)), dma((4,)),
        ],
        name="layer",
        compiler_params=pltpu.CompilerParams(
            collective_id=0, has_side_effects=True, vmem_limit_bytes=40 * 2**20
        ),
    )(tokens[0], grad_out[0], w_in[0], w_out[0], router, slot_scale[None, :])
    combined, grad_tokens, rows_x, rows_z, hidden, dact, grad_route, grad_scale = out

    def over_images(left, right):
        return mm_tn(left, right).astype(BF16)[None]

    return (
        combined[None],
        grad_tokens[None],
        grad_route.T,
        grad_scale[:, 0],
        over_images(rows_x, dact),
        over_images(hidden, rows_z),
    )


def solution(mesh):
    return jax.shard_map(
        shards,
        mesh=mesh,
        in_specs=(
            P("img", "tok", None),
            P("img", "tok", None),
            P(),
            P(),
            P("img", None, "tok"),
            P("img", "tok", None),
        ),
        out_specs=(
            P("img", "tok", None),
            P("img", "tok", None),
            P(),
            P(),
            P("img", None, "tok"),
            P("img", "tok", None),
        ),
        check_vma=False,
    )
```

```python
import jax
import jax.numpy as jnp
from jax import lax
from jax.experimental import pallas as pl
from jax.experimental.pallas import tpu as pltpu
from jax.sharding import PartitionSpec as P

EPSILON = 1e-06
ROOT_HALF = 0.7071067811865476
DENSITY = 0.3989422804014327
MESH = pl.DeviceIdType.MESH
F32 = jnp.float32
BF16 = jnp.bfloat16
D = 1280
HALF = 640
E = 64
M = 128
H = 1024
PIECE = 384
LIMIT = 51.5


def mm(a, b):
    return lax.dot_general(a, b, (((1,), (0,)), ((), ())), preferred_element_type=F32)


def mm_nt(a, b):
    return lax.dot_general(a, b, (((1,), (1,)), ((), ())), preferred_element_type=F32)


def mm_tn(a, b):
    return lax.dot_general(a, b, (((0,), (0,)), ((), ())), preferred_element_type=F32)


def pick(rows, cols):
    n = rows.shape[0]
    at = lax.broadcasted_iota(jnp.int32, (n, cols), 1)
    return jnp.where(at == rows, 1.0, 0.0).astype(BF16)


def to_row(col):
    n = col.shape[0]
    same = lax.broadcasted_iota(jnp.int32, (n, n), 0) == lax.broadcasted_iota(jnp.int32, (n, n), 1)
    return jnp.sum(jnp.where(same, col, 0.0), 0, keepdims=True)


def to_col(row):
    n = row.shape[1]
    same = lax.broadcasted_iota(jnp.int32, (n, n), 0) == lax.broadcasted_iota(jnp.int32, (n, n), 1)
    return jnp.sum(jnp.where(same, row, 0.0), 1, keepdims=True)


def layer(
    tokens_h, gout_h, w1_h, w2_h, router_h, scale_h,
    combined_ref, gtok_ref, groute_ref, gscale_ref, xt_ref, z_ref, ht_ref, dact_ref,
    tok, gout, w1, w2, router_v, scale_v, pack_m, unpack_m,
    part_tx, part_rx, den_tx, den_rx, own_a, sib_a, msg_tx, msg_rx, swap_tx, x_v, z_v, hid, dact,
    slope, own_b, swap2_tx, swap2_rx, swap3_tx, swap3_rx, sum_tx, sum_rx,
    ar_tx, ar_rx1, ar_rx2, ar_rx3,
    load_sem, pair_ss, pair_rs, a2a_ss, a2a_rs, ar_ss, ar_rs,
):
    img = lax.axis_index("img")
    t = lax.axis_index("tok")
    half = img // 64
    core = lax.rem(img, 2)
    idx = lax.rem(img, 64) // 2
    same = half == core
    sib = {"img": img + 1 - 2 * core, "tok": t}
    partner = {"img": img, "tok": 1 - t}

    def chip(m):
        return {"img": core * 64 + m * 2 + half, "tok": t}

    x_lo = lax.rem(img // 8, 2)
    y = lax.rem(img // 2, 4)
    z = img // 16
    mine = x_lo * 16 + core * 8 + t * 4 + y
    base = img - x_lo * 8 - core - y * 2

    def near(p):
        there = base + (p // 16) * 8 + lax.rem(p, 4) * 2 + lax.rem(p // 8, 2)
        return {"img": there, "tok": lax.rem(p // 4, 2)}

    def along_z(v):
        return {"img": img + (v - z) * 16, "tok": t}

    loads = [
        pltpu.make_async_copy(src, dst, load_sem.at[i])
        for i, (src, dst) in enumerate((
            (router_h, router_v), (scale_h, scale_v), (tokens_h, tok), (gout_h, gout), (w1_h, w1), (w2_h, w2)
        ))
    ]
    for load in loads:
        load.start()

    barrier = pltpu.get_barrier_semaphore()

    def greet(dev):
        pl.semaphore_signal(barrier, inc=1, device_id=dev, device_id_type=MESH)

    def greet_two(j, c):
        greet(chip(lax.rem(j + idx, 32)))
        greet(near(lax.rem(j + mine, 32)))
        return c

    lax.fori_loop(1, 32, greet_two, 0)
    for d in range(1, 8):
        greet(along_z(lax.rem(z + d, 8)))

    @pl.when(jnp.logical_not(same))
    def _():
        greet(chip(idx))

    row = lax.broadcasted_iota(jnp.int32, (256, 1), 0)
    m_of = lax.rem(row // 8 + idx, 32)
    side, u, v = (row // 4) % 2, (row // 2) % 2, row % 2
    w = jnp.where(u == core, 0, 1)
    pack_m[...] = pick(side * 128 + w * 64 + 2 * m_of + v, 256)
    w, side, m_of, u = row // 128, (row // 64) % 2, (row // 2) % 32, row % 2
    v = jnp.where(w == 0, core, 1 - core)
    unpack_m[...] = pick(m_of * 8 + side * 4 + u * 2 + v, 256)

    pairs = []

    def send(src, dst, dev):
        n = len(pairs)
        c = pltpu.make_async_remote_copy(
            src_ref=src, dst_ref=dst, send_sem=pair_ss.at[n], recv_sem=pair_rs.at[n],
            device_id=dev, device_id_type=MESH,
        )
        c.start()
        pairs.append(c)
        return c

    def spread(way, own, other):
        rows = jnp.concatenate([own[:, :HALF], other[:, :HALF], own[:, HALF:], other[:, HALF:]], 0)

        def chunk(q, c):
            at = pl.ds(pl.multiple_of(q * 128, 128), 128)
            block = mm(pack_m[at, :], rows).astype(BF16).reshape(16, 8, HALF)
            msg_tx[way, pl.ds(pl.multiple_of(q * 16, 16), 16)] = block

            def one(m, c):
                @pl.when(jnp.logical_or(m > 0, jnp.logical_not(same)))
                def _():
                    pltpu.make_async_remote_copy(
                        src_ref=msg_tx.at[way, m], dst_ref=msg_rx.at[way, idx],
                        send_sem=a2a_ss.at[way], recv_sem=a2a_rs.at[way],
                        device_id=chip(lax.rem(m + idx, 32)), device_id_type=MESH,
                    ).start()

                @pl.when(jnp.logical_and(m == 0, same))
                def _():
                    pltpu.make_async_copy(msg_tx.at[way, 0], msg_rx.at[way, idx], a2a_rs.at[way]).start()

                return c

            lax.fori_loop(q * 16, q * 16 + 16, one, 0)
            return c

        lax.fori_loop(0, 2, chunk, 0)

    def landed(way):
        pltpu.make_async_copy(msg_rx.at[way], msg_rx.at[way], a2a_rs.at[way]).wait()

    def left_tx(way):
        @pl.when(same)
        def _():
            sent = msg_tx.at[way, pl.ds(0, 31)]
            pltpu.make_async_copy(sent, sent, a2a_ss.at[way]).wait()

        @pl.when(jnp.logical_not(same))
        def _():
            pltpu.make_async_copy(msg_tx.at[way], msg_tx.at[way], a2a_ss.at[way]).wait()

    def gather(way, w):
        rows = msg_rx[way].reshape(256, HALF)
        out = mm(unpack_m[w * 128:w * 128 + 128, :], rows)
        return out[0:E], out[E:]

    loads[0].wait()
    loads[1].wait()
    router_b = router_v[...]
    router_t = router_b.astype(F32)
    inv_p = lax.rsqrt(jnp.sum(router_t * router_t, 1, keepdims=True) + EPSILON)
    scale = to_col(scale_v[...])
    column = inv_p * scale
    loads[2].wait()
    tok_f = tok[...].astype(F32)
    inv_x = to_row(lax.rsqrt(jnp.sum(tok_f * tok_f, 1, keepdims=True) + EPSILON))
    logit = mm_nt(router_b, tok[...]) * inv_x * column
    expo = jnp.exp(logit)
    den_part = jnp.sum(expo, 1, keepdims=True)
    den_row = to_row(den_part)
    den_tx[...] = jnp.broadcast_to(jnp.concatenate([den_row, den_row], 1), (8, 128))
    pw = expo.astype(BF16)
    numer = mm(pw, tok[...])
    part_tx[0:E, :] = numer.astype(BF16)

    pl.semaphore_wait(barrier, 31 + 31 + 7 + jnp.where(same, 0, 1))

    c_den = send(den_tx, den_rx, partner)
    c_num = send(part_tx.at[0:E], part_rx.at[0:E], partner)
    comb = expo / jnp.sum(expo, 0, keepdims=True)
    comb_b = comb.astype(BF16)
    loads[3].wait()
    dys = mm(comb_b, gout[...])
    part_tx[E:, :] = dys.astype(BF16)
    c_dys = send(part_tx.at[E:], part_rx.at[E:], partner)
    c_den.wait_recv()
    den = den_part + to_col(den_rx[0:1, 0:E])
    c_num.wait_recv()
    own_a[0:E, :] = ((numer + part_rx[0:E, :].astype(F32)) / den).astype(BF16)
    c_s1 = send(own_a.at[0:E], sib_a.at[0:E], sib)
    c_s1.wait_recv()
    spread(0, own_a[0:E, :], sib_a[0:E, :])
    c_dys.wait_recv()
    own_a[E:, :] = (dys + part_rx[E:, :].astype(F32)).astype(BF16)
    c_s2 = send(own_a.at[E:], sib_a.at[E:], sib)
    c_s2.wait_recv()
    spread(1, own_a[E:, :], sib_a[E:, :])

    def arrive(way, rows):
        lo = (way % 2) * E
        landed(way)
        left, right = gather(way, 1)
        swap_tx[lo:lo + E, :HALF] = left.astype(BF16)
        swap_tx[lo:lo + E, HALF:] = right.astype(BF16)
        c = send(swap_tx.at[lo:lo + E], rows.at[E:], sib)
        left, right = gather(way, 0)
        rows[0:E, :HALF] = left.astype(BF16)
        rows[0:E, HALF:] = right.astype(BF16)
        c.wait_recv()

    arrive(0, x_v)
    loads[4].wait()
    loads[5].wait()

    def expert_in(n, c):
        at = pl.ds(pl.multiple_of(n * 256, 256), 256)
        act = mm(x_v[...], w1[:, at])
        phi = 0.5 * (1.0 + lax.erf(act * ROOT_HALF))
        hid[:, at] = (act * phi).astype(BF16)
        slope[:, at] = phi + act * jnp.exp(-0.5 * act * act) * DENSITY
        return c

    lax.fori_loop(0, H // 256, expert_in, 0)

    def expert_out(n, c):
        at = pl.ds(pl.multiple_of(n * 256, 256), 256)
        part = mm(hid[...], w2[:, at]).astype(BF16)
        own_b[0:E, at] = part[0:E]
        swap2_tx[0:E, at] = part[E:]
        return c

    lax.fori_loop(0, D // 256, expert_out, 0)
    c_w2 = send(swap2_tx.at[0:E], swap2_rx.at[0:E], sib)
    c_w2.wait_recv()
    spread(2, own_b[0:E, :], swap2_rx[0:E, :])
    arrive(1, z_v)

    def expert_back(n, c):
        at = pl.ds(pl.multiple_of(n * 256, 256), 256)
        dh = mm_nt(z_v[...], w2[at, :])
        dact[:, at] = (dh * slope[:, at]).astype(BF16)
        return c

    lax.fori_loop(0, H // 256, expert_back, 0)

    def expert_back_in(n, c):
        at = pl.ds(pl.multiple_of(n * 256, 256), 256)
        part = mm_nt(dact[...], w1[at, :]).astype(BF16)
        own_b[E:, at] = part[0:E]
        swap2_tx[E:, at] = part[E:]
        return c

    lax.fori_loop(0, D // 256, expert_back_in, 0)
    c_w3 = send(swap2_tx.at[E:], swap2_rx.at[E:], sib)
    c_w3.wait_recv()
    spread(3, own_b[E:, :], swap2_rx[E:, :])

    def returned(way):
        lo = (way % 2) * E
        landed(way)
        left, right = gather(way, 1)
        swap3_tx[lo:lo + E, :HALF] = left.astype(BF16)
        swap3_tx[lo:lo + E, HALF:] = right.astype(BF16)
        c = send(swap3_tx.at[lo:lo + E], swap3_rx.at[lo:lo + E], sib)
        left, right = gather(way, 0)
        c.wait_recv()
        rows = jnp.concatenate([left, right], 1) + swap3_rx[lo:lo + E, :].astype(F32)
        sum_tx[lo:lo + E, :] = rows.astype(BF16)
        return rows, send(sum_tx.at[lo:lo + E], sum_rx.at[lo:lo + E], partner)

    rows, c_sum = returned(2)
    c_sum.wait_recv()
    ys = (rows + sum_rx[0:E, :].astype(F32)).astype(BF16)
    dcomb = mm_nt(ys, gout[...])
    dlc = comb * (dcomb - jnp.sum(comb * dcomb, 0, keepdims=True))
    combined_ref[...] = mm_tn(comb_b, ys).astype(BF16)
    rows, c_sum = returned(3)
    c_sum.wait_recv()
    dxs = (rows + sum_rx[E:, :].astype(F32)).astype(BF16)
    ddisp = mm_nt(dxs, tok[...])
    dxs_f = dxs.astype(F32)
    corr = jnp.sum(own_a[0:E, :].astype(F32) * dxs_f, 1, keepdims=True)
    grad_l = expo / den * (ddisp - corr) + dlc
    grad_q = (grad_l * column * inv_x).astype(BF16)
    outer = mm(grad_q, tok[...])
    wide = jnp.concatenate([outer, jnp.zeros((E, 4 * PIECE - D), F32)], 1).astype(BF16)
    for p in range(32):
        r, q = p // 4, p % 4
        ar_tx[p] = wide[8 * r:8 * r + 8, PIECE * q:PIECE * q + PIECE]

    def scatter(j, c):
        p = lax.rem(mine + j, 32)
        pltpu.make_async_remote_copy(
            src_ref=ar_tx.at[p], dst_ref=ar_rx1.at[mine], send_sem=ar_ss.at[0], recv_sem=ar_rs.at[0],
            device_id=near(p), device_id_type=MESH,
        ).start()
        return c

    lax.fori_loop(1, 32, scatter, 0)
    ar_rx1[mine] = ar_tx[mine]

    signal = jnp.sum(grad_l * logit, 0, keepdims=True)
    coef = to_col(inv_x * inv_x * signal)
    scaled = (dxs_f / den).astype(BF16)
    weights = jnp.concatenate([pw, grad_q], 0)
    values = jnp.concatenate([scaled, router_b], 0)
    gtok_ref[...] = (mm_tn(weights, values) - coef * tok_f).astype(BF16)

    def counted(ref, n, sem):
        pltpu.make_async_copy(ref.at[0:n], ref.at[0:n], sem).wait()

    def total_of(rx, n):
        acc = rx[0].astype(F32)
        for j in range(1, n):
            acc = acc + rx[j].astype(F32)
        return acc.astype(BF16)

    counted(ar_rx1, 31, ar_rs.at[0])
    ar_rx2[z] = total_of(ar_rx1, 32)
    for d in range(1, 8):
        pltpu.make_async_remote_copy(
            src_ref=ar_rx2.at[z], dst_ref=ar_rx2.at[z], send_sem=ar_ss.at[1], recv_sem=ar_rs.at[1],
            device_id=along_z(lax.rem(z + d, 8)), device_id_type=MESH,
        ).start()

    xt_ref[...] = x_v[...].T
    dact_ref[...] = dact[...]
    counted(ar_rx2, 7, ar_rs.at[1])
    ar_rx3[mine] = total_of(ar_rx2, 8)

    def collect(j, c):
        pltpu.make_async_remote_copy(
            src_ref=ar_rx3.at[mine], dst_ref=ar_rx3.at[mine], send_sem=ar_ss.at[2], recv_sem=ar_rs.at[2],
            device_id=near(lax.rem(mine + j, 32)), device_id_type=MESH,
        ).start()
        return c

    lax.fori_loop(1, 32, collect, 0)
    ht_ref[...] = hid[...].T
    z_ref[...] = z_v[...]
    for way in range(4):
        left_tx(way)
    for c in pairs:
        c.wait_send()
    counted(ar_tx, 31, ar_ss.at[0])
    counted(ar_rx2, 7, ar_ss.at[1])
    counted(ar_rx3, 31, ar_rs.at[2])
    counted(ar_rx3, 31, ar_ss.at[2])
    whole = jnp.concatenate(
        [jnp.concatenate([ar_rx3[4 * r + q] for q in range(4)], 1)[:, :D] for r in range(8)], 0
    ).astype(F32)
    total = jnp.sum(whole * router_t, 1, keepdims=True)
    groute_ref[...] = whole - inv_p * inv_p * total * router_t
    gscale_ref[...] = to_row(total / scale)


def finish(
    combined_v, gtok_v, groute_v, gscale_v, xt_ref, z_ref, ht_ref, dact_ref,
    combined_h, gtok_h, groute_h, gscale_h, g1_h, g2_h, g1, g2, sem,
):
    copies = []

    def out(src, dst):
        c = pltpu.make_async_copy(src, dst, sem.at[len(copies)])
        c.start()
        copies.append(c)

    def product(left, right, g, g_h, n):
        for i in range(n):
            at = pl.ds(i * 256, 256)
            g[at, :] = mm(left[at, :], right[...]).astype(BF16)
            out(g.at[at], g_h.at[at])

    product(xt_ref, dact_ref, g1, g1_h, 5)
    out(combined_v, combined_h)
    out(gtok_v, gtok_h)
    out(groute_v, groute_h)
    out(gscale_v, gscale_h)
    product(ht_ref, z_ref, g2, g2_h, 4)
    for c in copies:
        c.wait()


def shards(tokens, grad_out, router, slot_scale, w_in, w_out):
    hbm = pl.BlockSpec(memory_space=pltpu.HBM)
    vmem = pl.BlockSpec(memory_space=pltpu.VMEM)
    rows = pltpu.VMEM((128, D), BF16)
    half_rows = pltpu.VMEM((128, H), BF16)
    msgs = pltpu.VMEM((4, 32, 8, HALF), BF16)
    pieces = pltpu.VMEM((32, 8, PIECE), BF16)
    dma = pltpu.SemaphoreType.DMA
    shapes = [
        jax.ShapeDtypeStruct((M, D), BF16),
        jax.ShapeDtypeStruct((M, D), BF16),
        jax.ShapeDtypeStruct((E, D), F32),
        jax.ShapeDtypeStruct((1, E), F32),
    ]
    factors = [
        jax.ShapeDtypeStruct((D, 128), BF16),
        jax.ShapeDtypeStruct((128, D), BF16),
        jax.ShapeDtypeStruct((H, 128), BF16),
        jax.ShapeDtypeStruct((128, H), BF16),
    ]
    grads = [jax.ShapeDtypeStruct((D, H), BF16), jax.ShapeDtypeStruct((H, D), BF16)]
    out = pl.pallas_call(
        layer,
        out_shape=shapes + factors,
        in_specs=[hbm] * 6,
        out_specs=[vmem] * 8,
        scratch_shapes=[
            rows, rows, pltpu.VMEM((D, H), BF16), pltpu.VMEM((H, D), BF16),
            pltpu.VMEM((E, D), BF16), pltpu.VMEM((1, E), F32),
            pltpu.VMEM((256, 256), BF16), pltpu.VMEM((256, 256), BF16),
            rows, rows, pltpu.VMEM((8, 128), F32), pltpu.VMEM((8, 128), F32),
            rows, rows, msgs, msgs, rows, rows, rows, half_rows, half_rows,
            pltpu.VMEM((128, H), F32), rows, rows, rows, rows, rows, rows, rows,
            pieces, pieces, pltpu.VMEM((8, 8, PIECE), BF16), pieces,
            dma((6,)), dma((13,)), dma((13,)), dma((4,)), dma((4,)), dma((3,)), dma((3,)),
        ],
        name="layer",
        compiler_params=pltpu.CompilerParams(
            collective_id=0, has_side_effects=True, vmem_limit_bytes=int(LIMIT * 2**20)
        ),
    )(tokens[0], grad_out[0], w_in[0], w_out[0], router.T, slot_scale[None, :])
    combined, grad_tokens, grad_route, grad_scale, grad_w_in, grad_w_out = pl.pallas_call(
        finish,
        out_shape=shapes + grads,
        in_specs=[vmem] * 8,
        out_specs=[hbm] * 6,
        scratch_shapes=[pltpu.VMEM((D, H), BF16), pltpu.VMEM((H, D), BF16), dma((13,))],
        name="finish",
        compiler_params=pltpu.CompilerParams(vmem_limit_bytes=20 * 2**20),
    )(*out)
    return (
        combined[None],
        grad_tokens[None],
        grad_route.T,
        grad_scale[0],
        grad_w_in[None],
        grad_w_out[None],
    )


def solution(mesh):
    return jax.shard_map(
        shards,
        mesh=mesh,
        in_specs=(
            P("img", "tok", None),
            P("img", "tok", None),
            P(),
            P(),
            P("img", None, "tok"),
            P("img", "tok", None),
        ),
        out_specs=(
            P("img", "tok", None),
            P("img", "tok", None),
            P(),
            P(),
            P("img", None, "tok"),
            P("img", "tok", None),
        ),
        check_vma=False,
    )
```

```python
import jax
import jax.numpy as jnp
from jax import lax
from jax.experimental import pallas as pl
from jax.experimental.pallas import tpu as pltpu
from jax.sharding import PartitionSpec as P

EPSILON = 1e-06
ROOT_HALF = 0.7071067811865476
DENSITY = 0.3989422804014327
MESH = pl.DeviceIdType.MESH
F32 = jnp.float32
BF16 = jnp.bfloat16
D = 1280
HALF = 640
E = 64
C = 32
M = 128
H = 1024
PIECE = 384
LIMIT = 51.6


def mm(a, b):
    return lax.dot_general(a, b, (((1,), (0,)), ((), ())), preferred_element_type=F32)


def mm_nt(a, b):
    return lax.dot_general(a, b, (((1,), (1,)), ((), ())), preferred_element_type=F32)


def mm_tn(a, b):
    return lax.dot_general(a, b, (((0,), (0,)), ((), ())), preferred_element_type=F32)


def pick(rows, cols):
    n = rows.shape[0]
    at = lax.broadcasted_iota(jnp.int32, (n, cols), 1)
    return jnp.where(at == rows, 1.0, 0.0).astype(BF16)


def to_row(col):
    n = col.shape[0]
    same = lax.broadcasted_iota(jnp.int32, (n, n), 0) == lax.broadcasted_iota(jnp.int32, (n, n), 1)
    return jnp.sum(jnp.where(same, col, 0.0), 0, keepdims=True)


def to_col(row):
    n = row.shape[1]
    same = lax.broadcasted_iota(jnp.int32, (n, n), 0) == lax.broadcasted_iota(jnp.int32, (n, n), 1)
    return jnp.sum(jnp.where(same, row, 0.0), 1, keepdims=True)


def layer(
    tokens_h, gout_h, w1_h, w2_h, router_h, scale_h,
    combined_ref, gtok_ref, groute_ref, gscale_ref, xt_ref, z_ref, ht_ref, dact_ref,
    tok_all, gout, w1, w2, router_v, scale_v, pack_out, unpack_out, pack_back, unpack_back,
    part_tx, part_rx, den_tx, den_rx, info_tx, info_rx, own_a, sib_a, msg_tx, msg_rx, swap_tx, x_v, z_v,
    hid, dact, slope, own_b, swap2_tx, swap2_rx, swap3_tx, swap3_rx, ys_v, dlc_tx, dlc_rx,
    gd_v, gq_tx, gq_rx, sig_tx, sig_rx, ar_tx, ar_rx1, ar_rx2, ar_rx3,
    load_sem, pair_ss, pair_rs, a2a_ss, a2a_rs, ar_ss, ar_rs,
):
    img = lax.axis_index("img")
    t = lax.axis_index("tok")
    half = img >> 6
    core = img & 1
    idx = (img >> 1) & 31
    selfish = jnp.logical_and(half == core, (idx & 1) == t)
    sib = {"img": img + 1 - 2 * core, "tok": t}
    partner = {"img": img, "tok": 1 - t}
    tok = tok_all.at[0:M]

    def expert_dev(j):
        chip = ((((j & 15) + (idx >> 1)) & 15) << 1) + t
        return {"img": (core << 6) + (chip << 1) + half, "tok": t ^ (j >> 4)}

    def image_dev(j):
        return {"img": (core << 6) + (((j + idx) & 31) << 1) + half, "tok": idx & 1}

    z = img >> 4
    spot = (img & 8) + (core << 2) + ((img >> 1) & 3)
    mine = (t << 4) + spot

    def near(p):
        there = (z << 4) + (p & 8) + ((p & 3) << 1) + ((p >> 2) & 1)
        return {"img": there, "tok": p >> 4}

    def along_z(v):
        return {"img": (img & 15) + (v << 4), "tok": t}

    loads = [
        pltpu.make_async_copy(src, dst, load_sem.at[i])
        for i, (src, dst) in enumerate((
            (router_h, router_v), (scale_h, scale_v), (tokens_h, tok), (gout_h, gout), (w1_h, w1), (w2_h, w2)
        ))
    ]
    for load in loads:
        load.start()

    barrier = pltpu.get_barrier_semaphore()

    def greet(dev):
        pl.semaphore_signal(barrier, inc=1, device_id=dev, device_id_type=MESH)

    def greet_all(j, c):
        greet(expert_dev(j))
        greet(image_dev(j))
        greet(near((j + mine) & 31))
        return c

    lax.fori_loop(1, 32, greet_all, 0)
    for d in range(1, 8):
        greet(along_z((z + d) & 7))

    @pl.when(jnp.logical_not(selfish))
    def _():
        greet(expert_dev(0))
        greet(image_dev(0))

    row = lax.broadcasted_iota(jnp.int32, (128, 1), 0)
    q, side, u, v = ((row >> 3) + (idx >> 1)) & 15, (row >> 2) & 1, (row >> 1) & 1, row & 1
    pack_out[...] = pick(side * 64 + (u ^ core) * C + 2 * q + v, 128)
    w, side, q, u = row >> 6, (row >> 5) & 1, (row >> 1) & 15, row & 1
    at = lax.broadcasted_iota(jnp.int32, (128, 256), 1)
    here = (at & 247) == q * 16 + side * 4 + u * 2 + (core ^ w)
    unpack_back[...] = jnp.where(here, 1.0, 0.0).astype(BF16)
    row = lax.broadcasted_iota(jnp.int32, (256, 1), 0)
    m_of, side, u, v = ((row >> 3) + idx) & 31, (row >> 2) & 1, (row >> 1) & 1, row & 1
    pack_back[...] = pick(side * 128 + (u ^ core) * E + 2 * m_of + v, 256)
    w, side, m_of, u = row >> 7, (row >> 6) & 1, (row >> 1) & 31, row & 1
    unpack_out[...] = pick(m_of * 8 + side * 4 + u * 2 + (core ^ w), 256)

    pairs = []

    def send(src, dst, dev):
        n = len(pairs)
        c = pltpu.make_async_remote_copy(
            src_ref=src, dst_ref=dst, send_sem=pair_ss.at[n], recv_sem=pair_rs.at[n],
            device_id=dev, device_id_type=MESH,
        )
        c.start()
        pairs.append(c)
        return c

    def quarters(own, other):
        return jnp.concatenate([own[:, :HALF], other[:, :HALF], own[:, HALF:], other[:, HALF:]], 0)

    def post(way, first, dev, slot):
        def one(m, c):
            pltpu.make_async_remote_copy(
                src_ref=msg_tx.at[way, m], dst_ref=msg_rx.at[way, slot],
                send_sem=a2a_ss.at[way], recv_sem=a2a_rs.at[way],
                device_id=dev(m), device_id_type=MESH,
            ).start()
            return c

        lax.fori_loop(max(first, 1), first + 16, one, 0)
        if first == 0:
            @pl.when(selfish)
            def _():
                pltpu.make_async_copy(msg_tx.at[way, 0], msg_rx.at[way, slot], a2a_rs.at[way]).start()

            @pl.when(jnp.logical_not(selfish))
            def _():
                one(0, 0)

    def to_experts(way, own, other):
        block = mm(pack_out[...], quarters(own, other)).astype(BF16).reshape(16, 8, HALF)
        msg_tx[way, 0:16] = block
        msg_tx[way, 16:32] = block
        post(way, 0, expert_dev, idx)
        post(way, 16, expert_dev, idx)

    def to_images(way, own, other):
        rows = quarters(own, other)
        for q in range(2):
            block = mm(pack_back[q * 128:q * 128 + 128, :], rows).astype(BF16)
            msg_tx[way, q * 16:q * 16 + 16] = block.reshape(16, 8, HALF)
            post(way, q * 16, image_dev, (idx & 30) + t)

    def landed(way):
        pltpu.make_async_copy(msg_rx.at[way], msg_rx.at[way], a2a_rs.at[way]).wait()

    def left_tx(way):
        @pl.when(selfish)
        def _():
            sent = msg_tx.at[way, pl.ds(0, 31)]
            pltpu.make_async_copy(sent, sent, a2a_ss.at[way]).wait()

        @pl.when(jnp.logical_not(selfish))
        def _():
            pltpu.make_async_copy(msg_tx.at[way], msg_tx.at[way], a2a_ss.at[way]).wait()

    def gather(way, w):
        order = (unpack_out if way < 2 else unpack_back)
        n = order.shape[0] // 2
        out = mm(order[w * n:w * n + n, :], msg_rx[way].reshape(256, HALF))
        return out[0:n // 2], out[n // 2:]

    loads[0].wait()
    loads[1].wait()
    row = lax.broadcasted_iota(jnp.int32, (E, 1), 0)
    expert = ((row & 31) >> 1) * 4 + ((row >> 5) ^ t) * 2 + (row & 1)
    router_b = mm(pick(expert, E), router_v[...]).astype(BF16)
    router_t = router_b.astype(F32)
    at = lax.broadcasted_iota(jnp.int32, (E, E), 1)
    scale = jnp.sum(jnp.where(at == expert, scale_v[...], 0.0), 1, keepdims=True)
    column = lax.rsqrt(jnp.sum(router_t * router_t, 1, keepdims=True) + EPSILON) * scale
    loads[2].wait()
    tok_f = tok[...].astype(F32)
    inv_x = to_row(lax.rsqrt(jnp.sum(tok_f * tok_f, 1, keepdims=True) + EPSILON))
    logit = mm_nt(router_b, tok[...]) * inv_x * column
    expo = jnp.exp(logit)
    den_part = jnp.sum(expo, 1, keepdims=True)
    den_row = to_row(den_part)
    den_tx[...] = jnp.broadcast_to(jnp.concatenate([den_row, den_row], 1), (8, 128))
    pw = expo.astype(BF16)
    numer = mm(pw, tok[...])
    part_tx[0:C, :] = numer[C:].astype(BF16)

    pl.semaphore_wait(barrier, 3 * 31 + 7 + jnp.where(selfish, 0, 2))

    c_den = send(den_tx, den_rx, partner)
    c_num = send(part_tx.at[0:C], part_rx.at[0:C], partner)
    comb = expo / jnp.sum(expo, 0, keepdims=True)
    comb_b = comb.astype(BF16)
    loads[3].wait()
    dys = mm(comb_b, gout[...])
    part_tx[C:, :] = dys[C:].astype(BF16)
    c_dys = send(part_tx.at[C:], part_rx.at[C:], partner)
    c_tok = send(tok, tok_all.at[M:], partner)
    info_tx[0:C, :] = logit[C:]
    info_tx[C:, :] = jnp.broadcast_to(inv_x, (8, M))
    c_info = send(info_tx, info_rx, partner)
    c_den.wait_recv()
    den = den_part[0:C] + to_col(den_rx[0:1, 0:E])[C:]
    c_num.wait_recv()
    own_a[0:C, :] = ((numer[0:C] + part_rx[0:C, :].astype(F32)) / den).astype(BF16)
    c_s1 = send(own_a.at[0:C], sib_a.at[0:C], sib)
    c_s1.wait_recv()
    to_experts(0, own_a[0:C, :], sib_a[0:C, :])
    c_dys.wait_recv()
    own_a[C:, :] = (dys[0:C] + part_rx[C:, :].astype(F32)).astype(BF16)
    c_s2 = send(own_a.at[C:], sib_a.at[C:], sib)
    c_s2.wait_recv()
    to_experts(1, own_a[C:, :], sib_a[C:, :])

    def arrive(way, rows):
        lo = (way % 2) * E
        landed(way)
        left, right = gather(way, 1)
        swap_tx[lo:lo + E, :HALF] = left.astype(BF16)
        swap_tx[lo:lo + E, HALF:] = right.astype(BF16)
        c = send(swap_tx.at[lo:lo + E], rows.at[E:], sib)
        left, right = gather(way, 0)
        rows[0:E, :HALF] = left.astype(BF16)
        rows[0:E, HALF:] = right.astype(BF16)
        c.wait_recv()

    arrive(0, x_v)
    loads[4].wait()
    loads[5].wait()

    def expert_in(n, c):
        at = pl.ds(pl.multiple_of(n * 256, 256), 256)
        act = mm(x_v[...], w1[:, at])
        phi = 0.5 * (1.0 + lax.erf(act * ROOT_HALF))
        hid[:, at] = (act * phi).astype(BF16)
        slope[:, at] = phi + act * jnp.exp(-0.5 * act * act) * DENSITY
        return c

    lax.fori_loop(0, H // 256, expert_in, 0, unroll=True)

    def expert_out(n, c):
        at = pl.ds(pl.multiple_of(n * 256, 256), 256)
        part = mm(hid[...], w2[:, at]).astype(BF16)
        own_b[0:E, at] = part[0:E]
        swap2_tx[0:E, at] = part[E:]
        return c

    lax.fori_loop(0, D // 256, expert_out, 0, unroll=True)
    c_w2 = send(swap2_tx.at[0:E], swap2_rx.at[0:E], sib)
    c_w2.wait_recv()
    to_images(2, own_b[0:E, :], swap2_rx[0:E, :])
    arrive(1, z_v)

    def expert_back(n, c):
        at = pl.ds(pl.multiple_of(n * 256, 256), 256)
        dh = mm_nt(z_v[...], w2[at, :])
        dact[:, at] = (dh * slope[:, at]).astype(BF16)
        return c

    lax.fori_loop(0, H // 256, expert_back, 0, unroll=True)

    def expert_back_in(n, c):
        at = pl.ds(pl.multiple_of(n * 256, 256), 256)
        part = mm_nt(dact[...], w1[at, :]).astype(BF16)
        own_b[E:, at] = part[0:E]
        swap2_tx[E:, at] = part[E:]
        return c

    lax.fori_loop(0, D // 256, expert_back_in, 0, unroll=True)
    c_w3 = send(swap2_tx.at[E:], swap2_rx.at[E:], sib)
    c_w3.wait_recv()
    to_images(3, own_b[E:, :], swap2_rx[E:, :])

    def returned(way):
        lo = (way % 2) * C
        landed(way)
        left, right = gather(way, 1)
        swap3_tx[lo:lo + C, :HALF] = left.astype(BF16)
        swap3_tx[lo:lo + C, HALF:] = right.astype(BF16)
        c = send(swap3_tx.at[lo:lo + C], swap3_rx.at[lo:lo + C], sib)
        left, right = gather(way, 0)
        c.wait_recv()
        return (jnp.concatenate([left, right], 1) + swap3_rx[lo:lo + C, :].astype(F32)).astype(BF16)

    ys_v[0:C, :] = returned(2)
    c_ys = send(ys_v.at[0:C], ys_v.at[C:], partner)
    c_info.wait_recv()
    logit_o, inv_o = info_rx[0:C, :], info_rx[C:C + 1, :]
    expo_o = jnp.exp(logit_o)
    share, share_o = expo[0:C] / den, expo_o / den
    factor, factor_o = column[0:C] * inv_x, column[0:C] * inv_o
    c_ys.wait_recv()
    ys = ys_v[...]
    dcomb = mm_nt(ys, gout[...])
    dlc = comb * (dcomb - jnp.sum(comb * dcomb, 0, keepdims=True))
    dlc_tx[...] = dlc[C:]
    c_dlc = send(dlc_tx, dlc_rx, partner)
    combined_ref[...] = mm_tn(comb_b, ys).astype(BF16)
    c_tok.wait_recv()
    dxs = returned(3)
    c_dlc.wait_recv()
    ddisp, ddisp_o = mm_nt(dxs, tok[...]), mm_nt(dxs, tok_all[M:, :])
    corr = jnp.sum(share * ddisp, 1, keepdims=True) + jnp.sum(share_o * ddisp_o, 1, keepdims=True)
    grad_l = share * (ddisp - corr) + dlc[0:C]
    grad_o = share_o * (ddisp_o - corr) + dlc_rx[...]
    grad_q, grad_qo = (grad_l * factor).astype(BF16), (grad_o * factor_o).astype(BF16)
    outer = mm(jnp.concatenate([grad_q, grad_qo], 1), tok_all[...])
    wide = jnp.concatenate([outer, jnp.zeros((C, 4 * PIECE - D), F32)], 1).astype(BF16)
    for p in range(16):
        r, q = p // 4, p % 4
        ar_tx[p] = wide[8 * r:8 * r + 8, PIECE * q:PIECE * q + PIECE]

    def scatter(j, c):
        p = (spot + j) & 15
        pltpu.make_async_remote_copy(
            src_ref=ar_tx.at[p], dst_ref=ar_rx1.at[spot], send_sem=ar_ss.at[0], recv_sem=ar_rs.at[0],
            device_id=near((t << 4) + p), device_id_type=MESH,
        ).start()
        return c

    lax.fori_loop(1, 16, scatter, 0)
    ar_rx1[spot] = ar_tx[spot]

    gd_v[0:C, :] = (dxs.astype(F32) / den).astype(BF16)
    c_gd = send(gd_v.at[0:C], gd_v.at[C:], partner)
    gq_tx[...] = grad_qo
    c_gq = send(gq_tx, gq_rx, partner)
    sig_tx[...] = jnp.broadcast_to(jnp.sum(grad_o * logit_o, 0, keepdims=True), (8, M))
    c_sig = send(sig_tx, sig_rx, partner)
    signal = jnp.sum(grad_l * logit[0:C], 0, keepdims=True)

    def counted(ref, n, sem):
        pltpu.make_async_copy(ref.at[0:n], ref.at[0:n], sem).wait()

    def total_of(rx, n):
        acc = rx[0].astype(F32)
        for j in range(1, n):
            acc = acc + rx[j].astype(F32)
        return acc.astype(BF16)

    counted(ar_rx1, 15, ar_rs.at[0])
    ar_rx2[z] = total_of(ar_rx1, 16)
    for d in range(1, 8):
        pltpu.make_async_remote_copy(
            src_ref=ar_rx2.at[z], dst_ref=ar_rx2.at[z], send_sem=ar_ss.at[1], recv_sem=ar_rs.at[1],
            device_id=along_z((z + d) & 7), device_id_type=MESH,
        ).start()

    xt_ref[...] = x_v[...].T
    dact_ref[...] = dact[...]
    counted(ar_rx2, 7, ar_rs.at[1])
    ar_rx3[mine] = total_of(ar_rx2, 8)

    def collect(j, c):
        pltpu.make_async_remote_copy(
            src_ref=ar_rx3.at[mine], dst_ref=ar_rx3.at[mine], send_sem=ar_ss.at[2], recv_sem=ar_rs.at[2],
            device_id=near((mine + j) & 31), device_id_type=MESH,
        ).start()
        return c

    lax.fori_loop(1, 32, collect, 0)
    ht_ref[...] = hid[...].T
    z_ref[...] = z_v[...]
    router_f = router_v[...].astype(F32)
    inv_p = lax.rsqrt(jnp.sum(router_f * router_f, 1, keepdims=True) + EPSILON)
    c_gd.wait_recv()
    c_gq.wait_recv()
    c_sig.wait_recv()
    coef = to_col(inv_x * inv_x * (signal + sig_rx[0:1, :]))
    weights = jnp.concatenate([pw, grad_q, gq_rx[...]], 0)
    values = jnp.concatenate([gd_v[...], router_b], 0)
    gtok_ref[...] = (mm_tn(weights, values) - coef * tok[...].astype(F32)).astype(BF16)
    for way in range(4):
        left_tx(way)
    for c in pairs:
        c.wait_send()
    counted(ar_tx, 15, ar_ss.at[0])
    counted(ar_rx2, 7, ar_ss.at[1])
    counted(ar_rx3, 31, ar_rs.at[2])
    counted(ar_rx3, 31, ar_ss.at[2])
    whole = jnp.concatenate(
        [jnp.concatenate([ar_rx3[4 * r + q] for q in range(4)], 1)[:, :D] for r in range(8)], 0
    )
    row = lax.broadcasted_iota(jnp.int32, (E, 1), 0)
    whole = mm(pick(((row >> 1) & 1) * C + (row >> 2) * 2 + (row & 1), E), whole)
    total = jnp.sum(whole * router_f, 1, keepdims=True)
    groute_ref[...] = whole - inv_p * inv_p * total * router_f
    gscale_ref[...] = to_row(total) / scale_v[...]


def finish(
    combined_v, gtok_v, groute_v, gscale_v, xt_ref, z_ref, ht_ref, dact_ref,
    combined_h, gtok_h, groute_h, gscale_h, g1_h, g2_h, g1, g2, sem,
):
    copies = []

    def out(src, dst):
        c = pltpu.make_async_copy(src, dst, sem.at[len(copies)])
        c.start()
        copies.append(c)

    def product(left, right, g, g_h, n):
        for i in range(n):
            at = pl.ds(i * 256, 256)
            g[at, :] = mm(left[at, :], right[...]).astype(BF16)
            out(g.at[at], g_h.at[at])

    out(combined_v, combined_h)
    out(gtok_v, gtok_h)
    out(groute_v, groute_h)
    out(gscale_v, gscale_h)
    product(xt_ref, dact_ref, g1, g1_h, 5)
    product(ht_ref, z_ref, g2, g2_h, 4)
    for c in copies:
        c.wait()


def shards(tokens, grad_out, router, slot_scale, w_in, w_out):
    hbm = pl.BlockSpec(memory_space=pltpu.HBM)
    vmem = pl.BlockSpec(memory_space=pltpu.VMEM)
    rows = pltpu.VMEM((128, D), BF16)
    few = pltpu.VMEM((E, D), BF16)
    tile = pltpu.VMEM((8, 128), F32)
    half_rows = pltpu.VMEM((128, H), BF16)
    msgs = pltpu.VMEM((4, 32, 8, HALF), BF16)
    dma = pltpu.SemaphoreType.DMA
    shapes = [
        jax.ShapeDtypeStruct((M, D), BF16),
        jax.ShapeDtypeStruct((M, D), BF16),
        jax.ShapeDtypeStruct((E, D), F32),
        jax.ShapeDtypeStruct((1, E), F32),
    ]
    factors = [
        jax.ShapeDtypeStruct((D, 128), BF16),
        jax.ShapeDtypeStruct((128, D), BF16),
        jax.ShapeDtypeStruct((H, 128), BF16),
        jax.ShapeDtypeStruct((128, H), BF16),
    ]
    grads = [jax.ShapeDtypeStruct((D, H), BF16), jax.ShapeDtypeStruct((H, D), BF16)]
    out = pl.pallas_call(
        layer,
        out_shape=shapes + factors,
        in_specs=[hbm] * 6,
        out_specs=[vmem] * 8,
        scratch_shapes=[
            pltpu.VMEM((2 * M, D), BF16), rows, pltpu.VMEM((D, H), BF16), pltpu.VMEM((H, D), BF16),
            pltpu.VMEM((E, D), BF16), pltpu.VMEM((1, E), F32),
            pltpu.VMEM((128, 128), BF16), pltpu.VMEM((256, 256), BF16),
            pltpu.VMEM((256, 256), BF16), pltpu.VMEM((128, 256), BF16),
            few, few, tile, tile, pltpu.VMEM((40, M), F32), pltpu.VMEM((40, M), F32),
            few, few, msgs, msgs, rows, rows, rows,
            half_rows, half_rows, pltpu.VMEM((128, H), F32), rows, rows, rows, few, few, few,
            pltpu.VMEM((C, M), F32), pltpu.VMEM((C, M), F32),
            few, pltpu.VMEM((C, M), BF16), pltpu.VMEM((C, M), BF16), tile, tile,
            pltpu.VMEM((16, 8, PIECE), BF16), pltpu.VMEM((16, 8, PIECE), BF16),
            pltpu.VMEM((8, 8, PIECE), BF16), pltpu.VMEM((32, 8, PIECE), BF16),
            dma((6,)), dma((18,)), dma((18,)), dma((4,)), dma((4,)), dma((3,)), dma((3,)),
        ],
        name="layer",
        compiler_params=pltpu.CompilerParams(
            collective_id=0, has_side_effects=True, vmem_limit_bytes=int(LIMIT * 2**20)
        ),
    )(tokens[0], grad_out[0], w_in[0], w_out[0], router.T, slot_scale[None, :])
    combined, grad_tokens, grad_route, grad_scale, grad_w_in, grad_w_out = pl.pallas_call(
        finish,
        out_shape=shapes + grads,
        in_specs=[vmem] * 8,
        out_specs=[hbm] * 6,
        scratch_shapes=[pltpu.VMEM((D, H), BF16), pltpu.VMEM((H, D), BF16), dma((13,))],
        name="finish",
        compiler_params=pltpu.CompilerParams(vmem_limit_bytes=20 * 2**20),
    )(*out)
    return (
        combined[None],
        grad_tokens[None],
        grad_route.T,
        grad_scale[0],
        grad_w_in[None],
        grad_w_out[None],
    )


def solution(mesh):
    return jax.shard_map(
        shards,
        mesh=mesh,
        in_specs=(
            P("img", "tok", None),
            P("img", "tok", None),
            P(),
            P(),
            P("img", None, "tok"),
            P("img", "tok", None),
        ),
        out_specs=(
            P("img", "tok", None),
            P("img", "tok", None),
            P(),
            P(),
            P("img", None, "tok"),
            P("img", "tok", None),
        ),
        check_vma=False,
    )
```

```python
import jax
import jax.numpy as jnp
from jax import lax
from jax.experimental import pallas as pl
from jax.experimental.pallas import tpu as pltpu
from jax.sharding import PartitionSpec as P

EPSILON = 1e-06
ROOT_HALF = 0.7071067811865476
DENSITY = 0.3989422804014327
MESH = pl.DeviceIdType.MESH
F32 = jnp.float32
BF16 = jnp.bfloat16
D = 1280
HALF = 640
E = 64
C = 32
M = 128
H = 1024
PIECE = 384
LIMIT = 51.6


def mm(a, b):
    return lax.dot_general(a, b, (((1,), (0,)), ((), ())), preferred_element_type=F32)


def mm_nt(a, b):
    return lax.dot_general(a, b, (((1,), (1,)), ((), ())), preferred_element_type=F32)


def mm_tn(a, b):
    return lax.dot_general(a, b, (((0,), (0,)), ((), ())), preferred_element_type=F32)


def pick(rows, cols):
    n = rows.shape[0]
    at = lax.broadcasted_iota(jnp.int32, (n, cols), 1)
    return jnp.where(at == rows, 1.0, 0.0).astype(BF16)


def to_row(col):
    n = col.shape[0]
    same = lax.broadcasted_iota(jnp.int32, (n, n), 0) == lax.broadcasted_iota(jnp.int32, (n, n), 1)
    return jnp.sum(jnp.where(same, col, 0.0), 0, keepdims=True)


def to_col(row):
    n = row.shape[1]
    same = lax.broadcasted_iota(jnp.int32, (n, n), 0) == lax.broadcasted_iota(jnp.int32, (n, n), 1)
    return jnp.sum(jnp.where(same, row, 0.0), 1, keepdims=True)


def layer(
    tokens_h, gout_h, w1_h, w2_h, router_h, scale_h,
    combined_ref, gtok_ref, groute_ref, gscale_ref, xt_ref, z_ref, ht_ref, dact_ref,
    tok_all, gout_all, w1, w2, router_v, scale_v, pack_out, unpack_out, pack_back, unpack_back,
    part_tx, part_rx, den_tx, den_rx, info_tx, info_rx, own_a, sib_a, msg_tx, msg_rx, swap_tx, x_v, z_v,
    hid, dact, slope, own_b, swap2_tx, swap2_rx, swap3_tx, swap3_rx, ys_v, row_tx, row_rx,
    gd_v, gq_tx, gq_rx, sig_tx, sig_rx, ar_tx, ar_rx1, ar_rx2, ar_rx3,
    load_sem, pair_ss, pair_rs, a2a_ss, a2a_rs, ar_ss, ar_rs,
):
    img = lax.axis_index("img")
    t = lax.axis_index("tok")
    half = img >> 6
    core = img & 1
    idx = (img >> 1) & 31
    selfish = jnp.logical_and(half == core, (idx & 1) == t)
    sib = {"img": img + 1 - 2 * core, "tok": t}
    partner = {"img": img, "tok": 1 - t}
    tok = tok_all.at[0:M]
    gout = gout_all.at[0:M]

    def expert_dev(j):
        chip = ((((j & 15) + (idx >> 1)) & 15) << 1) + t
        return {"img": (core << 6) + (chip << 1) + half, "tok": t ^ (j >> 4)}

    def image_dev(j):
        return {"img": (core << 6) + (((j + idx) & 31) << 1) + half, "tok": idx & 1}

    z = img >> 4
    spot = (img & 8) + (core << 2) + ((img >> 1) & 3)
    mine = (t << 4) + spot

    def near(p):
        there = (z << 4) + (p & 8) + ((p & 3) << 1) + ((p >> 2) & 1)
        return {"img": there, "tok": p >> 4}

    def along_z(v):
        return {"img": (img & 15) + (v << 4), "tok": t}

    loads = [
        pltpu.make_async_copy(src, dst, load_sem.at[i])
        for i, (src, dst) in enumerate((
            (router_h, router_v), (scale_h, scale_v), (tokens_h, tok), (gout_h, gout), (w1_h, w1), (w2_h, w2)
        ))
    ]
    for load in loads:
        load.start()

    barrier = pltpu.get_barrier_semaphore()

    def greet(dev):
        pl.semaphore_signal(barrier, inc=1, device_id=dev, device_id_type=MESH)

    def greet_all(j, c):
        greet(expert_dev(j))
        greet(image_dev(j))
        greet(near((j + mine) & 31))
        return c

    lax.fori_loop(1, 32, greet_all, 0)
    for d in range(1, 8):
        greet(along_z((z + d) & 7))

    @pl.when(jnp.logical_not(selfish))
    def _():
        greet(expert_dev(0))
        greet(image_dev(0))

    row = lax.broadcasted_iota(jnp.int32, (128, 1), 0)
    q, side, u, v = ((row >> 3) + (idx >> 1)) & 15, (row >> 2) & 1, (row >> 1) & 1, row & 1
    pack_out[...] = pick(side * 64 + (u ^ core) * C + 2 * q + v, 128)
    w, side, q, u = row >> 6, (row >> 5) & 1, (row >> 1) & 15, row & 1
    at = lax.broadcasted_iota(jnp.int32, (128, 256), 1)
    here = (at & 247) == q * 16 + side * 4 + u * 2 + (core ^ w)
    unpack_back[...] = jnp.where(here, 1.0, 0.0).astype(BF16)
    row = lax.broadcasted_iota(jnp.int32, (256, 1), 0)
    m_of, side, u, v = ((row >> 3) + idx) & 31, (row >> 2) & 1, (row >> 1) & 1, row & 1
    pack_back[...] = pick(side * 128 + (u ^ core) * E + 2 * m_of + v, 256)
    w, side, m_of, u = row >> 7, (row >> 6) & 1, (row >> 1) & 31, row & 1
    unpack_out[...] = pick(m_of * 8 + side * 4 + u * 2 + (core ^ w), 256)

    pairs = []

    def send(src, dst, dev):
        n = len(pairs)
        c = pltpu.make_async_remote_copy(
            src_ref=src, dst_ref=dst, send_sem=pair_ss.at[n], recv_sem=pair_rs.at[n],
            device_id=dev, device_id_type=MESH,
        )
        c.start()
        pairs.append(c)
        return c

    def quarters(own, other):
        return jnp.concatenate([own[:, :HALF], other[:, :HALF], own[:, HALF:], other[:, HALF:]], 0)

    def post(way, first, dev, slot):
        def one(m, c):
            pltpu.make_async_remote_copy(
                src_ref=msg_tx.at[way, m], dst_ref=msg_rx.at[way, slot],
                send_sem=a2a_ss.at[way], recv_sem=a2a_rs.at[way],
                device_id=dev(m), device_id_type=MESH,
            ).start()
            return c

        lax.fori_loop(max(first, 1), first + 16, one, 0)
        if first == 0:
            @pl.when(selfish)
            def _():
                pltpu.make_async_copy(msg_tx.at[way, 0], msg_rx.at[way, slot], a2a_rs.at[way]).start()

            @pl.when(jnp.logical_not(selfish))
            def _():
                one(0, 0)

    def to_experts(way, own, other):
        block = mm(pack_out[...], quarters(own, other)).astype(BF16).reshape(16, 8, HALF)
        msg_tx[way, 0:16] = block
        msg_tx[way, 16:32] = block
        post(way, 0, expert_dev, idx)
        post(way, 16, expert_dev, idx)

    def to_images(way, own, other):
        rows = quarters(own, other)
        for q in range(2):
            block = mm(pack_back[q * 128:q * 128 + 128, :], rows).astype(BF16)
            msg_tx[way, q * 16:q * 16 + 16] = block.reshape(16, 8, HALF)
            post(way, q * 16, image_dev, (idx & 30) + t)

    def landed(way):
        pltpu.make_async_copy(msg_rx.at[way], msg_rx.at[way], a2a_rs.at[way]).wait()

    def left_tx(way):
        @pl.when(selfish)
        def _():
            sent = msg_tx.at[way, pl.ds(0, 31)]
            pltpu.make_async_copy(sent, sent, a2a_ss.at[way]).wait()

        @pl.when(jnp.logical_not(selfish))
        def _():
            pltpu.make_async_copy(msg_tx.at[way], msg_tx.at[way], a2a_ss.at[way]).wait()

    def gather(way, w):
        order = (unpack_out if way < 2 else unpack_back)
        n = order.shape[0] // 2
        out = mm(order[w * n:w * n + n, :], msg_rx[way].reshape(256, HALF))
        return out[0:n // 2], out[n // 2:]

    loads[0].wait()
    loads[1].wait()
    row = lax.broadcasted_iota(jnp.int32, (E, 1), 0)
    expert = ((row & 31) >> 1) * 4 + ((row >> 5) ^ t) * 2 + (row & 1)
    router_b = mm(pick(expert, E), router_v[...]).astype(BF16)
    router_t = router_b.astype(F32)
    at = lax.broadcasted_iota(jnp.int32, (E, E), 1)
    scale = jnp.sum(jnp.where(at == expert, scale_v[...], 0.0), 1, keepdims=True)
    column = lax.rsqrt(jnp.sum(router_t * router_t, 1, keepdims=True) + EPSILON) * scale
    loads[2].wait()
    tok_f = tok[...].astype(F32)
    inv_x = to_row(lax.rsqrt(jnp.sum(tok_f * tok_f, 1, keepdims=True) + EPSILON))
    logit = mm_nt(router_b, tok[...]) * inv_x * column
    expo = jnp.exp(logit)
    den_part = jnp.sum(expo, 1, keepdims=True)
    den_row = to_row(den_part)
    den_tx[...] = jnp.broadcast_to(jnp.concatenate([den_row, den_row], 1), (8, 128))
    pw = expo.astype(BF16)
    numer = mm(pw, tok[...])
    part_tx[0:C, :] = numer[C:].astype(BF16)

    pl.semaphore_wait(barrier, 3 * 31 + 7 + jnp.where(selfish, 0, 2))

    c_den = send(den_tx, den_rx, partner)
    c_num = send(part_tx.at[0:C], part_rx.at[0:C], partner)
    row_sum = jnp.sum(expo, 0, keepdims=True)
    comb = expo / row_sum
    comb_b = comb.astype(BF16)
    loads[3].wait()
    dys = mm(comb_b, gout[...])
    part_tx[C:, :] = dys[C:].astype(BF16)
    c_dys = send(part_tx.at[C:], part_rx.at[C:], partner)
    info_tx[0:C, :] = logit[C:]
    info_tx[C:C + 8, :] = jnp.broadcast_to(inv_x, (8, M))
    info_tx[C + 8:, :] = jnp.broadcast_to(row_sum, (8, M))
    c_info = send(info_tx, info_rx, partner)
    c_gout = send(gout, gout_all.at[M:], partner)
    c_den.wait_recv()
    den = den_part[0:C] + to_col(den_rx[0:1, 0:E])[C:]
    c_num.wait_recv()
    own_a[0:C, :] = ((numer[0:C] + part_rx[0:C, :].astype(F32)) / den).astype(BF16)
    c_s1 = send(own_a.at[0:C], sib_a.at[0:C], sib)
    c_s1.wait_recv()
    to_experts(0, own_a[0:C, :], sib_a[0:C, :])
    c_dys.wait_recv()
    own_a[C:, :] = (dys[0:C] + part_rx[C:, :].astype(F32)).astype(BF16)
    c_s2 = send(own_a.at[C:], sib_a.at[C:], sib)
    c_s2.wait_recv()
    to_experts(1, own_a[C:, :], sib_a[C:, :])
    c_tok = send(tok, tok_all.at[M:], partner)

    def arrive(way, rows):
        lo = (way % 2) * E
        landed(way)
        left, right = gather(way, 1)
        swap_tx[lo:lo + E, :HALF] = left.astype(BF16)
        swap_tx[lo:lo + E, HALF:] = right.astype(BF16)
        c = send(swap_tx.at[lo:lo + E], rows.at[E:], sib)
        left, right = gather(way, 0)
        rows[0:E, :HALF] = left.astype(BF16)
        rows[0:E, HALF:] = right.astype(BF16)
        c.wait_recv()

    arrive(0, x_v)
    loads[4].wait()
    loads[5].wait()

    def expert_in(n, c):
        at = pl.ds(pl.multiple_of(n * 256, 256), 256)
        act = mm(x_v[...], w1[:, at])
        phi = 0.5 * (1.0 + lax.erf(act * ROOT_HALF))
        hid[:, at] = (act * phi).astype(BF16)
        slope[:, at] = phi + act * jnp.exp(-0.5 * act * act) * DENSITY
        return c

    lax.fori_loop(0, H // 256, expert_in, 0, unroll=True)

    def expert_out(n, c):
        at = pl.ds(pl.multiple_of(n * 256, 256), 256)
        part = mm(hid[...], w2[:, at]).astype(BF16)
        own_b[0:E, at] = part[0:E]
        swap2_tx[0:E, at] = part[E:]
        return c

    lax.fori_loop(0, D // 256, expert_out, 0, unroll=True)
    c_w2 = send(swap2_tx.at[0:E], swap2_rx.at[0:E], sib)
    c_w2.wait_recv()
    to_images(2, own_b[0:E, :], swap2_rx[0:E, :])
    arrive(1, z_v)

    def expert_back(n, c):
        at = pl.ds(pl.multiple_of(n * 256, 256), 256)
        dh = mm_nt(z_v[...], w2[at, :])
        dact[:, at] = (dh * slope[:, at]).astype(BF16)
        return c

    lax.fori_loop(0, H // 256, expert_back, 0, unroll=True)

    def expert_back_in(n, c):
        at = pl.ds(pl.multiple_of(n * 256, 256), 256)
        part = mm_nt(dact[...], w1[at, :]).astype(BF16)
        own_b[E:, at] = part[0:E]
        swap2_tx[E:, at] = part[E:]
        return c

    lax.fori_loop(0, D // 256, expert_back_in, 0, unroll=True)
    c_w3 = send(swap2_tx.at[E:], swap2_rx.at[E:], sib)
    c_w3.wait_recv()
    to_images(3, own_b[E:, :], swap2_rx[E:, :])

    def returned(way):
        lo = (way % 2) * C
        landed(way)
        left, right = gather(way, 1)
        swap3_tx[lo:lo + C, :HALF] = left.astype(BF16)
        swap3_tx[lo:lo + C, HALF:] = right.astype(BF16)
        c = send(swap3_tx.at[lo:lo + C], swap3_rx.at[lo:lo + C], sib)
        left, right = gather(way, 0)
        c.wait_recv()
        return (jnp.concatenate([left, right], 1) + swap3_rx[lo:lo + C, :].astype(F32)).astype(BF16)

    ys_v[0:C, :] = returned(2)
    c_ys = send(ys_v.at[0:C], ys_v.at[C:], partner)
    c_info.wait_recv()
    logit_o, inv_o, sum_o = info_rx[0:C, :], info_rx[C:C + 1, :], info_rx[C + 8:C + 9, :]
    expo_o = jnp.exp(logit_o)
    comb_m, comb_o = comb[0:C], expo_o / sum_o
    c_gout.wait_recv()
    share, share_o = expo[0:C] / den, expo_o / den
    factor, factor_o = column[0:C] * inv_x, column[0:C] * inv_o
    ys = ys_v[0:C, :]
    dcomb, dcomb_o = mm_nt(ys, gout[...]), mm_nt(ys, gout_all[M:, :])
    row_own = jnp.sum(comb_m * dcomb, 0, keepdims=True)
    row_o = jnp.sum(comb_o * dcomb_o, 0, keepdims=True)
    row_tx[0:8, :] = jnp.broadcast_to(row_o, (8, M))
    row_tx[8:, :] = jnp.broadcast_to(row_own, (8, M))
    c_row = send(row_tx, row_rx, partner)
    c_tok.wait_recv()
    dxs = returned(3)
    c_row.wait_recv()
    dlc = comb_m * (dcomb - row_own - row_rx[0:1, :])
    dlc_o = comb_o * (dcomb_o - row_o - row_rx[8:9, :])
    ddisp, ddisp_o = mm_nt(dxs, tok[...]), mm_nt(dxs, tok_all[M:, :])
    corr = jnp.sum(share * ddisp, 1, keepdims=True) + jnp.sum(share_o * ddisp_o, 1, keepdims=True)
    grad_l = share * (ddisp - corr) + dlc
    grad_o = share_o * (ddisp_o - corr) + dlc_o
    grad_q, grad_qo = (grad_l * factor).astype(BF16), (grad_o * factor_o).astype(BF16)
    outer = mm(jnp.concatenate([grad_q, grad_qo], 1), tok_all[...])
    wide = jnp.concatenate([outer, jnp.zeros((C, 4 * PIECE - D), F32)], 1).astype(BF16)
    for p in range(16):
        r, q = p // 4, p % 4
        ar_tx[p] = wide[8 * r:8 * r + 8, PIECE * q:PIECE * q + PIECE]

    def scatter(j, c):
        p = (spot + j) & 15
        pltpu.make_async_remote_copy(
            src_ref=ar_tx.at[p], dst_ref=ar_rx1.at[spot], send_sem=ar_ss.at[0], recv_sem=ar_rs.at[0],
            device_id=near((t << 4) + p), device_id_type=MESH,
        ).start()
        return c

    lax.fori_loop(1, 16, scatter, 0)
    ar_rx1[spot] = ar_tx[spot]

    gd_v[0:C, :] = (dxs.astype(F32) / den).astype(BF16)
    c_gd = send(gd_v.at[0:C], gd_v.at[C:], partner)
    gq_tx[...] = grad_qo
    c_gq = send(gq_tx, gq_rx, partner)
    sig_tx[...] = jnp.broadcast_to(jnp.sum(grad_o * logit_o, 0, keepdims=True), (8, M))
    c_sig = send(sig_tx, sig_rx, partner)
    signal = jnp.sum(grad_l * logit[0:C], 0, keepdims=True)
    c_ys.wait_recv()
    combined_ref[...] = mm_tn(comb_b, ys_v[...]).astype(BF16)

    def counted(ref, n, sem):
        pltpu.make_async_copy(ref.at[0:n], ref.at[0:n], sem).wait()

    def total_of(rx, n):
        acc = rx[0].astype(F32)
        for j in range(1, n):
            acc = acc + rx[j].astype(F32)
        return acc.astype(BF16)

    counted(ar_rx1, 15, ar_rs.at[0])
    ar_rx2[z] = total_of(ar_rx1, 16)
    for d in range(1, 8):
        pltpu.make_async_remote_copy(
            src_ref=ar_rx2.at[z], dst_ref=ar_rx2.at[z], send_sem=ar_ss.at[1], recv_sem=ar_rs.at[1],
            device_id=along_z((z + d) & 7), device_id_type=MESH,
        ).start()

    xt_ref[...] = x_v[...].T
    dact_ref[...] = dact[...]
    counted(ar_rx2, 7, ar_rs.at[1])
    ar_rx3[mine] = total_of(ar_rx2, 8)

    def collect(j, c):
        pltpu.make_async_remote_copy(
            src_ref=ar_rx3.at[mine], dst_ref=ar_rx3.at[mine], send_sem=ar_ss.at[2], recv_sem=ar_rs.at[2],
            device_id=near((mine + j) & 31), device_id_type=MESH,
        ).start()
        return c

    lax.fori_loop(1, 32, collect, 0)
    ht_ref[...] = hid[...].T
    z_ref[...] = z_v[...]
    router_f = router_v[...].astype(F32)
    inv_p = lax.rsqrt(jnp.sum(router_f * router_f, 1, keepdims=True) + EPSILON)
    c_gd.wait_recv()
    c_gq.wait_recv()
    c_sig.wait_recv()
    coef = to_col(inv_x * inv_x * (signal + sig_rx[0:1, :]))
    weights = jnp.concatenate([pw, grad_q, gq_rx[...]], 0)
    values = jnp.concatenate([gd_v[...], router_b], 0)
    gtok_ref[...] = (mm_tn(weights, values) - coef * tok[...].astype(F32)).astype(BF16)
    for way in range(4):
        left_tx(way)
    for c in pairs:
        c.wait_send()
    counted(ar_tx, 15, ar_ss.at[0])
    counted(ar_rx2, 7, ar_ss.at[1])
    counted(ar_rx3, 31, ar_rs.at[2])
    counted(ar_rx3, 31, ar_ss.at[2])
    whole = jnp.concatenate(
        [jnp.concatenate([ar_rx3[4 * r + q] for q in range(4)], 1)[:, :D] for r in range(8)], 0
    )
    row = lax.broadcasted_iota(jnp.int32, (E, 1), 0)
    whole = mm(pick(((row >> 1) & 1) * C + (row >> 2) * 2 + (row & 1), E), whole)
    total = jnp.sum(whole * router_f, 1, keepdims=True)
    groute_ref[...] = whole - inv_p * inv_p * total * router_f
    gscale_ref[...] = to_row(total) / scale_v[...]


def finish(
    combined_v, gtok_v, groute_v, gscale_v, xt_ref, z_ref, ht_ref, dact_ref,
    combined_h, gtok_h, groute_h, gscale_h, g1_h, g2_h, g1, g2, sem,
):
    copies = []

    def out(src, dst):
        c = pltpu.make_async_copy(src, dst, sem.at[len(copies)])
        c.start()
        copies.append(c)

    def product(left, right, g, g_h, n):
        for i in range(n):
            at = pl.ds(i * 256, 256)
            g[at, :] = mm(left[at, :], right[...]).astype(BF16)
            out(g.at[at], g_h.at[at])

    out(combined_v, combined_h)
    out(gtok_v, gtok_h)
    out(groute_v, groute_h)
    out(gscale_v, gscale_h)
    product(xt_ref, dact_ref, g1, g1_h, 5)
    product(ht_ref, z_ref, g2, g2_h, 4)
    for c in copies:
        c.wait()


def shards(tokens, grad_out, router, slot_scale, w_in, w_out):
    hbm = pl.BlockSpec(memory_space=pltpu.HBM)
    vmem = pl.BlockSpec(memory_space=pltpu.VMEM)
    rows = pltpu.VMEM((128, D), BF16)
    few = pltpu.VMEM((E, D), BF16)
    tile = pltpu.VMEM((8, 128), F32)
    half_rows = pltpu.VMEM((128, H), BF16)
    msgs = pltpu.VMEM((4, 32, 8, HALF), BF16)
    dma = pltpu.SemaphoreType.DMA
    shapes = [
        jax.ShapeDtypeStruct((M, D), BF16),
        jax.ShapeDtypeStruct((M, D), BF16),
        jax.ShapeDtypeStruct((E, D), F32),
        jax.ShapeDtypeStruct((1, E), F32),
    ]
    factors = [
        jax.ShapeDtypeStruct((D, 128), BF16),
        jax.ShapeDtypeStruct((128, D), BF16),
        jax.ShapeDtypeStruct((H, 128), BF16),
        jax.ShapeDtypeStruct((128, H), BF16),
    ]
    grads = [jax.ShapeDtypeStruct((D, H), BF16), jax.ShapeDtypeStruct((H, D), BF16)]
    out = pl.pallas_call(
        layer,
        out_shape=shapes + factors,
        in_specs=[hbm] * 6,
        out_specs=[vmem] * 8,
        scratch_shapes=[
            pltpu.VMEM((2 * M, D), BF16), pltpu.VMEM((2 * M, D), BF16), pltpu.VMEM((D, H), BF16), pltpu.VMEM((H, D), BF16),
            pltpu.VMEM((E, D), BF16), pltpu.VMEM((1, E), F32),
            pltpu.VMEM((128, 128), BF16), pltpu.VMEM((256, 256), BF16),
            pltpu.VMEM((256, 256), BF16), pltpu.VMEM((128, 256), BF16),
            few, few, tile, tile, pltpu.VMEM((48, M), F32), pltpu.VMEM((48, M), F32),
            few, few, msgs, msgs, rows, rows, rows,
            half_rows, half_rows, pltpu.VMEM((128, H), F32), rows, rows, rows, few, few, few,
            pltpu.VMEM((16, M), F32), pltpu.VMEM((16, M), F32),
            few, pltpu.VMEM((C, M), BF16), pltpu.VMEM((C, M), BF16), tile, tile,
            pltpu.VMEM((16, 8, PIECE), BF16), pltpu.VMEM((16, 8, PIECE), BF16),
            pltpu.VMEM((8, 8, PIECE), BF16), pltpu.VMEM((32, 8, PIECE), BF16),
            dma((6,)), dma((19,)), dma((19,)), dma((4,)), dma((4,)), dma((3,)), dma((3,)),
        ],
        name="layer",
        compiler_params=pltpu.CompilerParams(
            collective_id=0, has_side_effects=True, vmem_limit_bytes=int(LIMIT * 2**20)
        ),
    )(*[
        pltpu.with_memory_space_constraint(x, pltpu.HBM)
        for x in (tokens[0], grad_out[0], w_in[0], w_out[0], router.T, slot_scale[None, :])
    ])
    combined, grad_tokens, grad_route, grad_scale, grad_w_in, grad_w_out = pl.pallas_call(
        finish,
        out_shape=shapes + grads,
        in_specs=[vmem] * 8,
        out_specs=[hbm] * 6,
        scratch_shapes=[pltpu.VMEM((D, H), BF16), pltpu.VMEM((H, D), BF16), dma((13,))],
        name="finish",
        compiler_params=pltpu.CompilerParams(vmem_limit_bytes=20 * 2**20),
    )(*out)
    return (
        combined[None],
        grad_tokens[None],
        grad_route.T,
        grad_scale[0],
        grad_w_in[None],
        grad_w_out[None],
    )


def solution(mesh):
    return jax.shard_map(
        shards,
        mesh=mesh,
        in_specs=(
            P("img", "tok", None),
            P("img", "tok", None),
            P(),
            P(),
            P("img", None, "tok"),
            P("img", "tok", None),
        ),
        out_specs=(
            P("img", "tok", None),
            P("img", "tok", None),
            P(),
            P(),
            P("img", None, "tok"),
            P("img", "tok", None),
        ),
        check_vma=False,
    )
```

```python
import jax
import jax.numpy as jnp
from jax import lax
from jax.experimental import pallas as pl
from jax.experimental.pallas import tpu as pltpu
from jax.sharding import PartitionSpec as P

EPSILON = 1e-06
ROOT_HALF = 0.7071067811865476
DENSITY = 0.3989422804014327
MESH = pl.DeviceIdType.MESH
F32 = jnp.float32
BF16 = jnp.bfloat16
D = 1280
HALF = 640
E = 64
C = 32
M = 128
H = 1024
PIECE = 384
LIMIT = 51.6


def mm(a, b):
    return lax.dot_general(a, b, (((1,), (0,)), ((), ())), preferred_element_type=F32)


def mm_nt(a, b):
    return lax.dot_general(a, b, (((1,), (1,)), ((), ())), preferred_element_type=F32)


def mm_tn(a, b):
    return lax.dot_general(a, b, (((0,), (0,)), ((), ())), preferred_element_type=F32)


def pick(rows, cols):
    n = rows.shape[0]
    at = lax.broadcasted_iota(jnp.int32, (n, cols), 1)
    return jnp.where(at == rows, 1.0, 0.0).astype(BF16)


def to_row(col):
    n = col.shape[0]
    same = lax.broadcasted_iota(jnp.int32, (n, n), 0) == lax.broadcasted_iota(jnp.int32, (n, n), 1)
    return jnp.sum(jnp.where(same, col, 0.0), 0, keepdims=True)


def to_col(row):
    n = row.shape[1]
    same = lax.broadcasted_iota(jnp.int32, (n, n), 0) == lax.broadcasted_iota(jnp.int32, (n, n), 1)
    return jnp.sum(jnp.where(same, row, 0.0), 1, keepdims=True)


def layer(
    tokens_h, gout_h, w1_h, w2_h, router_h, scale_h,
    combined_ref, gtok_ref, groute_ref, gscale_ref, xt_ref, z_ref, ht_ref, dact_ref,
    tok_all, gout_all, w1, w2, router_v, scale_v, pack_out, unpack_out, pack_back, unpack_back,
    part_tx, part_rx, den_tx, den_rx, info_tx, info_rx, own_a, sib_a, msg_tx, msg_rx, swap_tx, x_v, z_v,
    hid, dact, slope, own_b, swap2_tx, swap2_rx, swap3_tx, swap3_rx, ys_v, row_tx, row_rx,
    gd_v, gq_tx, gq_rx, sig_tx, sig_rx, ar_tx, ar_rx1, ar_rx2, ar_rx3,
    load_sem, pair_ss, pair_rs, a2a_ss, a2a_rs, ar_ss, ar_rs,
):
    img = lax.axis_index("img")
    t = lax.axis_index("tok")
    half = img >> 6
    core = img & 1
    idx = (img >> 1) & 31
    selfish = jnp.logical_and(half == core, (idx & 1) == t)
    sib = {"img": img + 1 - 2 * core, "tok": t}
    partner = {"img": img, "tok": 1 - t}
    tok = tok_all.at[0:M]
    gout = gout_all.at[0:M]

    def expert_dev(j):
        chip = ((((j & 15) + (idx >> 1)) & 15) << 1) + t
        return {"img": (core << 6) + (chip << 1) + half, "tok": t ^ (j >> 4)}

    def image_dev(j):
        return {"img": (core << 6) + (((j + idx) & 31) << 1) + half, "tok": idx & 1}

    z = img >> 4
    spot = (img & 8) + (core << 2) + ((img >> 1) & 3)
    mine = (t << 4) + spot

    def near(p):
        there = (z << 4) + (p & 8) + ((p & 3) << 1) + ((p >> 2) & 1)
        return {"img": there, "tok": p >> 4}

    def along_z(v):
        return {"img": (img & 15) + (v << 4), "tok": t}

    loads = [
        pltpu.make_async_copy(src, dst, load_sem.at[i])
        for i, (src, dst) in enumerate((
            (router_h, router_v), (scale_h, scale_v), (tokens_h, tok), (gout_h, gout), (w1_h, w1), (w2_h, w2)
        ))
    ]
    for load in loads:
        load.start()

    barrier = pltpu.get_barrier_semaphore()

    def greet(dev):
        pl.semaphore_signal(barrier, inc=1, device_id=dev, device_id_type=MESH)

    def greet_all(j, c):
        greet(expert_dev(j))
        greet(image_dev(j))
        greet(near((j + mine) & 31))
        return c

    lax.fori_loop(1, 32, greet_all, 0)
    for d in range(1, 8):
        greet(along_z((z + d) & 7))

    @pl.when(jnp.logical_not(selfish))
    def _():
        greet(expert_dev(0))
        greet(image_dev(0))

    row = lax.broadcasted_iota(jnp.int32, (128, 1), 0)
    q, side, u, v = ((row >> 3) + (idx >> 1)) & 15, (row >> 2) & 1, (row >> 1) & 1, row & 1
    pack_out[...] = pick(side * 64 + (u ^ core) * C + 2 * q + v, 128)
    w, side, q, u = row >> 6, (row >> 5) & 1, (row >> 1) & 15, row & 1
    at = lax.broadcasted_iota(jnp.int32, (128, 256), 1)
    here = (at & 247) == q * 16 + side * 4 + u * 2 + (core ^ w)
    unpack_back[...] = jnp.where(here, 1.0, 0.0).astype(BF16)
    row = lax.broadcasted_iota(jnp.int32, (256, 1), 0)
    m_of, side, u, v = ((row >> 3) + idx) & 31, (row >> 2) & 1, (row >> 1) & 1, row & 1
    pack_back[...] = pick(side * 128 + (u ^ core) * E + 2 * m_of + v, 256)
    w, side, m_of, u = row >> 7, (row >> 6) & 1, (row >> 1) & 31, row & 1
    unpack_out[...] = pick(m_of * 8 + side * 4 + u * 2 + (core ^ w), 256)

    pairs = []

    def send(src, dst, dev):
        n = len(pairs)
        c = pltpu.make_async_remote_copy(
            src_ref=src, dst_ref=dst, send_sem=pair_ss.at[n], recv_sem=pair_rs.at[n],
            device_id=dev, device_id_type=MESH,
        )
        c.start()
        pairs.append(c)
        return c

    def quarters(own, other):
        return jnp.concatenate([own[:, :HALF], other[:, :HALF], own[:, HALF:], other[:, HALF:]], 0)

    def post(way, first, dev, slot):
        def one(m, c):
            pltpu.make_async_remote_copy(
                src_ref=msg_tx.at[way, m], dst_ref=msg_rx.at[way, slot],
                send_sem=a2a_ss.at[way], recv_sem=a2a_rs.at[way],
                device_id=dev(m), device_id_type=MESH,
            ).start()
            return c

        lax.fori_loop(max(first, 1), first + 16, one, 0)
        if first == 0:
            @pl.when(selfish)
            def _():
                pltpu.make_async_copy(msg_tx.at[way, 0], msg_rx.at[way, slot], a2a_rs.at[way]).start()

            @pl.when(jnp.logical_not(selfish))
            def _():
                one(0, 0)

    def to_experts(way, own, other):
        block = mm(pack_out[...], quarters(own, other)).astype(BF16).reshape(16, 8, HALF)
        msg_tx[way, 0:16] = block
        msg_tx[way, 16:32] = block
        post(way, 0, expert_dev, idx)
        post(way, 16, expert_dev, idx)

    def to_images(way, own, other):
        rows = quarters(own, other)
        for q in range(2):
            block = mm(pack_back[q * 128:q * 128 + 128, :], rows).astype(BF16)
            msg_tx[way, q * 16:q * 16 + 16] = block.reshape(16, 8, HALF)
            post(way, q * 16, image_dev, (idx & 30) + t)

    def landed(way):
        pltpu.make_async_copy(msg_rx.at[way], msg_rx.at[way], a2a_rs.at[way]).wait()

    def left_tx(way):
        @pl.when(selfish)
        def _():
            sent = msg_tx.at[way, pl.ds(0, 31)]
            pltpu.make_async_copy(sent, sent, a2a_ss.at[way]).wait()

        @pl.when(jnp.logical_not(selfish))
        def _():
            pltpu.make_async_copy(msg_tx.at[way], msg_tx.at[way], a2a_ss.at[way]).wait()

    def gather(way, w):
        order = (unpack_out if way < 2 else unpack_back)
        n = order.shape[0] // 2
        out = mm(order[w * n:w * n + n, :], msg_rx[way].reshape(256, HALF))
        return out[0:n // 2], out[n // 2:]

    loads[0].wait()
    loads[1].wait()
    row = lax.broadcasted_iota(jnp.int32, (E, 1), 0)
    expert = ((row & 31) >> 1) * 4 + ((row >> 5) ^ t) * 2 + (row & 1)
    router_b = mm(pick(expert, E), router_v[...]).astype(BF16)
    router_t = router_b.astype(F32)
    at = lax.broadcasted_iota(jnp.int32, (E, E), 1)
    scale = jnp.sum(jnp.where(at == expert, scale_v[...], 0.0), 1, keepdims=True)
    column = lax.rsqrt(jnp.sum(router_t * router_t, 1, keepdims=True) + EPSILON) * scale
    loads[2].wait()
    tok_f = tok[...].astype(F32)
    inv_x = to_row(lax.rsqrt(jnp.sum(tok_f * tok_f, 1, keepdims=True) + EPSILON))
    logit = mm_nt(router_b, tok[...]) * inv_x * column
    expo = jnp.exp(logit)
    den_part = jnp.sum(expo, 1, keepdims=True)
    den_row = to_row(den_part)
    den_tx[...] = jnp.broadcast_to(jnp.concatenate([den_row, den_row], 1), (8, 128))
    pw = expo.astype(BF16)
    numer = mm(pw, tok[...])
    part_tx[0:C, :] = numer[C:].astype(BF16)

    pl.semaphore_wait(barrier, 3 * 31 + 7 + jnp.where(selfish, 0, 2))

    c_den = send(den_tx, den_rx, partner)
    c_num = send(part_tx.at[0:C], part_rx.at[0:C], partner)
    row_sum = jnp.sum(expo, 0, keepdims=True)
    comb = expo / row_sum
    comb_b = comb.astype(BF16)
    loads[3].wait()
    dys = mm(comb_b, gout[...])
    part_tx[C:, :] = dys[C:].astype(BF16)
    c_dys = send(part_tx.at[C:], part_rx.at[C:], partner)
    info_tx[0:C, :] = logit[C:]
    info_tx[C:C + 8, :] = jnp.broadcast_to(inv_x, (8, M))
    info_tx[C + 8:, :] = jnp.broadcast_to(row_sum, (8, M))
    c_info = send(info_tx, info_rx, partner)
    c_gout = send(gout, gout_all.at[M:], partner)
    c_den.wait_recv()
    den = den_part[0:C] + to_col(den_rx[0:1, 0:E])[C:]
    c_num.wait_recv()
    own_a[0:C, :] = ((numer[0:C] + part_rx[0:C, :].astype(F32)) / den).astype(BF16)
    c_s1 = send(own_a.at[0:C], sib_a.at[0:C], sib)
    c_s1.wait_recv()
    to_experts(0, own_a[0:C, :], sib_a[0:C, :])
    c_dys.wait_recv()
    own_a[C:, :] = (dys[0:C] + part_rx[C:, :].astype(F32)).astype(BF16)
    c_s2 = send(own_a.at[C:], sib_a.at[C:], sib)
    c_s2.wait_recv()
    to_experts(1, own_a[C:, :], sib_a[C:, :])
    c_tok = send(tok, tok_all.at[M:], partner)

    def arrive(way, rows):
        lo = (way % 2) * E
        landed(way)
        left, right = gather(way, 1)
        swap_tx[lo:lo + E, :HALF] = left.astype(BF16)
        swap_tx[lo:lo + E, HALF:] = right.astype(BF16)
        c = send(swap_tx.at[lo:lo + E], rows.at[E:], sib)
        left, right = gather(way, 0)
        rows[0:E, :HALF] = left.astype(BF16)
        rows[0:E, HALF:] = right.astype(BF16)
        c.wait_recv()

    arrive(0, x_v)
    loads[4].wait()
    loads[5].wait()

    def expert_in(n, c):
        at = pl.ds(pl.multiple_of(n * 256, 256), 256)
        act = mm(x_v[...], w1[:, at])
        phi = 0.5 * (1.0 + lax.erf(act * ROOT_HALF))
        hid[:, at] = (act * phi).astype(BF16)
        slope[:, at] = phi + act * jnp.exp(-0.5 * act * act) * DENSITY
        return c

    lax.fori_loop(0, H // 256, expert_in, 0, unroll=True)

    def expert_out(n, c):
        at = pl.ds(pl.multiple_of(n * 256, 256), 256)
        part = mm(hid[...], w2[:, at]).astype(BF16)
        own_b[0:E, at] = part[0:E]
        swap2_tx[0:E, at] = part[E:]
        return c

    lax.fori_loop(0, D // 256, expert_out, 0, unroll=True)
    c_w2 = send(swap2_tx.at[0:E], swap2_rx.at[0:E], sib)
    c_w2.wait_recv()
    to_images(2, own_b[0:E, :], swap2_rx[0:E, :])
    arrive(1, z_v)

    def expert_back(n, c):
        at = pl.ds(pl.multiple_of(n * 256, 256), 256)
        dh = mm_nt(z_v[...], w2[at, :])
        dact[:, at] = (dh * slope[:, at]).astype(BF16)
        return c

    lax.fori_loop(0, H // 256, expert_back, 0, unroll=True)

    def expert_back_in(n, c):
        at = pl.ds(pl.multiple_of(n * 256, 256), 256)
        part = mm_nt(dact[...], w1[at, :]).astype(BF16)
        own_b[E:, at] = part[0:E]
        swap2_tx[E:, at] = part[E:]
        return c

    lax.fori_loop(0, D // 256, expert_back_in, 0, unroll=True)
    c_w3 = send(swap2_tx.at[E:], swap2_rx.at[E:], sib)
    c_w3.wait_recv()
    to_images(3, own_b[E:, :], swap2_rx[E:, :])

    def returned(way):
        lo = (way % 2) * C
        landed(way)
        left, right = gather(way, 1)
        swap3_tx[lo:lo + C, :HALF] = left.astype(BF16)
        swap3_tx[lo:lo + C, HALF:] = right.astype(BF16)
        c = send(swap3_tx.at[lo:lo + C], swap3_rx.at[lo:lo + C], sib)
        left, right = gather(way, 0)
        c.wait_recv()
        return (jnp.concatenate([left, right], 1) + swap3_rx[lo:lo + C, :].astype(F32)).astype(BF16)

    ys_v[0:C, :] = returned(2)
    c_info.wait_recv()
    logit_o, inv_o, sum_o = info_rx[0:C, :], info_rx[C:C + 1, :], info_rx[C + 8:C + 9, :]
    expo_o = jnp.exp(logit_o)
    comb_m, comb_o = comb[0:C], expo_o / sum_o
    c_gout.wait_recv()
    share, share_o = expo[0:C] / den, expo_o / den
    factor, factor_o = column[0:C] * inv_x, column[0:C] * inv_o
    ys = ys_v[0:C, :]
    dcomb, dcomb_o = mm_nt(ys, gout[...]), mm_nt(ys, gout_all[M:, :])
    row_own = jnp.sum(comb_m * dcomb, 0, keepdims=True)
    row_o = jnp.sum(comb_o * dcomb_o, 0, keepdims=True)
    row_tx[0:8, :] = jnp.broadcast_to(row_o, (8, M))
    row_tx[8:, :] = jnp.broadcast_to(row_own, (8, M))
    c_row = send(row_tx, row_rx, partner)
    c_ys = send(ys_v.at[0:C], ys_v.at[C:], partner)
    c_tok.wait_recv()
    dxs = returned(3)
    c_row.wait_recv()
    dlc = comb_m * (dcomb - row_own - row_rx[0:1, :])
    dlc_o = comb_o * (dcomb_o - row_o - row_rx[8:9, :])
    ddisp, ddisp_o = mm_nt(dxs, tok[...]), mm_nt(dxs, tok_all[M:, :])
    corr = jnp.sum(share * ddisp, 1, keepdims=True) + jnp.sum(share_o * ddisp_o, 1, keepdims=True)
    grad_l = share * (ddisp - corr) + dlc
    grad_o = share_o * (ddisp_o - corr) + dlc_o
    grad_q, grad_qo = (grad_l * factor).astype(BF16), (grad_o * factor_o).astype(BF16)
    outer = mm(jnp.concatenate([grad_q, grad_qo], 1), tok_all[...])
    wide = jnp.concatenate([outer, jnp.zeros((C, 4 * PIECE - D), F32)], 1).astype(BF16)
    for p in range(16):
        r, q = p // 4, p % 4
        ar_tx[p] = wide[8 * r:8 * r + 8, PIECE * q:PIECE * q + PIECE]

    def scatter(j, c):
        p = (spot + j) & 15
        pltpu.make_async_remote_copy(
            src_ref=ar_tx.at[p], dst_ref=ar_rx1.at[spot], send_sem=ar_ss.at[0], recv_sem=ar_rs.at[0],
            device_id=near((t << 4) + p), device_id_type=MESH,
        ).start()
        return c

    lax.fori_loop(1, 16, scatter, 0)
    ar_rx1[spot] = ar_tx[spot]

    gd_v[0:C, :] = (dxs.astype(F32) / den).astype(BF16)
    c_gd = send(gd_v.at[0:C], gd_v.at[C:], partner)
    gq_tx[...] = grad_qo
    c_gq = send(gq_tx, gq_rx, partner)
    sig_tx[...] = jnp.broadcast_to(jnp.sum(grad_o * logit_o, 0, keepdims=True), (8, M))
    c_sig = send(sig_tx, sig_rx, partner)
    signal = jnp.sum(grad_l * logit[0:C], 0, keepdims=True)
    c_ys.wait_recv()
    combined_ref[...] = mm_tn(comb_b, ys_v[...]).astype(BF16)

    def counted(ref, n, sem):
        pltpu.make_async_copy(ref.at[0:n], ref.at[0:n], sem).wait()

    def total_of(rx, n):
        acc = rx[0].astype(F32)
        for j in range(1, n):
            acc = acc + rx[j].astype(F32)
        return acc.astype(BF16)

    counted(ar_rx1, 15, ar_rs.at[0])
    ar_rx2[z] = total_of(ar_rx1, 16)
    for d in range(1, 8):
        pltpu.make_async_remote_copy(
            src_ref=ar_rx2.at[z], dst_ref=ar_rx2.at[z], send_sem=ar_ss.at[1], recv_sem=ar_rs.at[1],
            device_id=along_z((z + d) & 7), device_id_type=MESH,
        ).start()

    xt_ref[...] = x_v[...].T
    dact_ref[...] = dact[...]
    counted(ar_rx2, 7, ar_rs.at[1])
    ar_rx3[mine] = total_of(ar_rx2, 8)

    def collect(j, c):
        pltpu.make_async_remote_copy(
            src_ref=ar_rx3.at[mine], dst_ref=ar_rx3.at[mine], send_sem=ar_ss.at[2], recv_sem=ar_rs.at[2],
            device_id=near((mine + j) & 31), device_id_type=MESH,
        ).start()
        return c

    lax.fori_loop(1, 32, collect, 0)
    ht_ref[...] = hid[...].T
    z_ref[...] = z_v[...]
    router_f = router_v[...].astype(F32)
    inv_p = lax.rsqrt(jnp.sum(router_f * router_f, 1, keepdims=True) + EPSILON)
    c_gd.wait_recv()
    c_gq.wait_recv()
    c_sig.wait_recv()
    coef = to_col(inv_x * inv_x * (signal + sig_rx[0:1, :]))
    weights = jnp.concatenate([pw, grad_q, gq_rx[...]], 0)
    values = jnp.concatenate([gd_v[...], router_b], 0)
    gtok_ref[...] = (mm_tn(weights, values) - coef * tok[...].astype(F32)).astype(BF16)
    for way in range(4):
        left_tx(way)
    for c in pairs:
        c.wait_send()
    counted(ar_tx, 15, ar_ss.at[0])
    counted(ar_rx2, 7, ar_ss.at[1])
    counted(ar_rx3, 31, ar_rs.at[2])
    counted(ar_rx3, 31, ar_ss.at[2])
    whole = jnp.concatenate(
        [jnp.concatenate([ar_rx3[4 * r + q] for q in range(4)], 1)[:, :D] for r in range(8)], 0
    )
    row = lax.broadcasted_iota(jnp.int32, (E, 1), 0)
    whole = mm(pick(((row >> 1) & 1) * C + (row >> 2) * 2 + (row & 1), E), whole)
    total = jnp.sum(whole * router_f, 1, keepdims=True)
    groute_ref[...] = whole - inv_p * inv_p * total * router_f
    gscale_ref[...] = to_row(total) / scale_v[...]


def finish(
    combined_v, gtok_v, groute_v, gscale_v, xt_ref, z_ref, ht_ref, dact_ref,
    combined_h, gtok_h, groute_h, gscale_h, g1_h, g2_h, g1, g2, sem,
):
    copies = []

    def out(src, dst):
        c = pltpu.make_async_copy(src, dst, sem.at[len(copies)])
        c.start()
        copies.append(c)

    def product(left, right, g, g_h, n):
        for i in range(n):
            at = pl.ds(i * 256, 256)
            g[at, :] = mm(left[at, :], right[...]).astype(BF16)
            out(g.at[at], g_h.at[at])

    out(combined_v, combined_h)
    out(gtok_v, gtok_h)
    out(groute_v, groute_h)
    out(gscale_v, gscale_h)
    product(xt_ref, dact_ref, g1, g1_h, 5)
    product(ht_ref, z_ref, g2, g2_h, 4)
    for c in copies:
        c.wait()


def shards(tokens, grad_out, router, slot_scale, w_in, w_out):
    hbm = pl.BlockSpec(memory_space=pltpu.HBM)
    vmem = pl.BlockSpec(memory_space=pltpu.VMEM)
    rows = pltpu.VMEM((128, D), BF16)
    few = pltpu.VMEM((E, D), BF16)
    tile = pltpu.VMEM((8, 128), F32)
    half_rows = pltpu.VMEM((128, H), BF16)
    msgs = pltpu.VMEM((4, 32, 8, HALF), BF16)
    dma = pltpu.SemaphoreType.DMA
    shapes = [
        jax.ShapeDtypeStruct((M, D), BF16),
        jax.ShapeDtypeStruct((M, D), BF16),
        jax.ShapeDtypeStruct((E, D), F32),
        jax.ShapeDtypeStruct((1, E), F32),
    ]
    factors = [
        jax.ShapeDtypeStruct((D, 128), BF16),
        jax.ShapeDtypeStruct((128, D), BF16),
        jax.ShapeDtypeStruct((H, 128), BF16),
        jax.ShapeDtypeStruct((128, H), BF16),
    ]
    grads = [jax.ShapeDtypeStruct((D, H), BF16), jax.ShapeDtypeStruct((H, D), BF16)]
    out = pl.pallas_call(
        layer,
        out_shape=shapes + factors,
        in_specs=[hbm] * 6,
        out_specs=[vmem] * 8,
        scratch_shapes=[
            pltpu.VMEM((2 * M, D), BF16), pltpu.VMEM((2 * M, D), BF16), pltpu.VMEM((D, H), BF16), pltpu.VMEM((H, D), BF16),
            pltpu.VMEM((E, D), BF16), pltpu.VMEM((1, E), F32),
            pltpu.VMEM((128, 128), BF16), pltpu.VMEM((256, 256), BF16),
            pltpu.VMEM((256, 256), BF16), pltpu.VMEM((128, 256), BF16),
            few, few, tile, tile, pltpu.VMEM((48, M), F32), pltpu.VMEM((48, M), F32),
            few, few, msgs, msgs, rows, rows, rows,
            half_rows, half_rows, pltpu.VMEM((128, H), F32), rows, rows, rows, few, few, few,
            pltpu.VMEM((16, M), F32), pltpu.VMEM((16, M), F32),
            few, pltpu.VMEM((C, M), BF16), pltpu.VMEM((C, M), BF16), tile, tile,
            pltpu.VMEM((16, 8, PIECE), BF16), pltpu.VMEM((16, 8, PIECE), BF16),
            pltpu.VMEM((8, 8, PIECE), BF16), pltpu.VMEM((32, 8, PIECE), BF16),
            dma((6,)), dma((19,)), dma((19,)), dma((4,)), dma((4,)), dma((3,)), dma((3,)),
        ],
        name="layer",
        compiler_params=pltpu.CompilerParams(
            collective_id=0, has_side_effects=True, vmem_limit_bytes=int(LIMIT * 2**20)
        ),
    )(*[
        pltpu.with_memory_space_constraint(x, pltpu.HBM)
        for x in (tokens[0], grad_out[0], w_in[0], w_out[0], router.T, slot_scale[None, :])
    ])
    combined, grad_tokens, grad_route, grad_scale, grad_w_in, grad_w_out = pl.pallas_call(
        finish,
        out_shape=shapes + grads,
        in_specs=[vmem] * 8,
        out_specs=[hbm] * 6,
        scratch_shapes=[pltpu.VMEM((D, H), BF16), pltpu.VMEM((H, D), BF16), dma((13,))],
        name="finish",
        compiler_params=pltpu.CompilerParams(vmem_limit_bytes=20 * 2**20),
    )(*out)
    return (
        combined[None],
        grad_tokens[None],
        grad_route.T,
        grad_scale[0],
        grad_w_in[None],
        grad_w_out[None],
    )


def solution(mesh):
    return jax.shard_map(
        shards,
        mesh=mesh,
        in_specs=(
            P("img", "tok", None),
            P("img", "tok", None),
            P(),
            P(),
            P("img", None, "tok"),
            P("img", "tok", None),
        ),
        out_specs=(
            P("img", "tok", None),
            P("img", "tok", None),
            P(),
            P(),
            P("img", None, "tok"),
            P("img", "tok", None),
        ),
        check_vma=False,
    )
```

```python
import jax
import jax.numpy as jnp
from jax import lax
from jax.experimental import pallas as pl
from jax.experimental.pallas import tpu as pltpu
from jax.sharding import PartitionSpec as P

EPSILON = 1e-06
ROOT_HALF = 0.7071067811865476
DENSITY = 0.3989422804014327
MESH = pl.DeviceIdType.MESH
F32 = jnp.float32
BF16 = jnp.bfloat16
D = 1280
HALF = 640
E = 64
C = 32
M = 128
H = 1024
PIECE = 384
LIMIT = 51.6


def mm(a, b):
    return lax.dot_general(a, b, (((1,), (0,)), ((), ())), preferred_element_type=F32)


def mm_nt(a, b):
    return lax.dot_general(a, b, (((1,), (1,)), ((), ())), preferred_element_type=F32)


def mm_tn(a, b):
    return lax.dot_general(a, b, (((0,), (0,)), ((), ())), preferred_element_type=F32)


def pick(rows, cols):
    n = rows.shape[0]
    at = lax.broadcasted_iota(jnp.int32, (n, cols), 1)
    return jnp.where(at == rows, 1.0, 0.0).astype(BF16)


def to_row(col):
    n = col.shape[0]
    same = lax.broadcasted_iota(jnp.int32, (n, n), 0) == lax.broadcasted_iota(jnp.int32, (n, n), 1)
    return jnp.sum(jnp.where(same, col, 0.0), 0, keepdims=True)


def to_col(row):
    n = row.shape[1]
    same = lax.broadcasted_iota(jnp.int32, (n, n), 0) == lax.broadcasted_iota(jnp.int32, (n, n), 1)
    return jnp.sum(jnp.where(same, row, 0.0), 1, keepdims=True)


def layer(
    tokens_h, gout_h, w1_h, w2_h, router_h, scale_h,
    combined_ref, gtok_ref, groute_ref, gscale_ref, xt_ref, z_ref, ht_ref, dact_ref,
    tok_all, gout_all, w1, w2, router_v, scale_v, pack_out, unpack_out, pack_back, unpack_back,
    part_tx, part_rx, den_tx, den_rx, info_tx, info_rx, own_a, sib_a, msg_tx, msg_rx, swap_tx, x_v, z_v,
    hid, dact, slope, own_b, swap2_tx, swap2_rx, swap3_tx, swap3_rx, ys_v, row_tx, row_rx,
    gd_v, gq_tx, gq_rx, sig_tx, sig_rx, ar_tx, ar_rx1, ar_rx2, ar_rx3,
    load_sem, pair_ss, pair_rs, a2a_ss, a2a_rs, ar_ss, ar_rs,
):
    img = lax.axis_index("img")
    t = lax.axis_index("tok")
    half = img >> 6
    core = img & 1
    idx = (img >> 1) & 31
    selfish = jnp.logical_and(half == core, (idx & 1) == t)
    sib = {"img": img + 1 - 2 * core, "tok": t}
    partner = {"img": img, "tok": 1 - t}
    tok = tok_all.at[0:M]
    gout = gout_all.at[0:M]

    def expert_dev(j):
        chip = ((((j & 15) + (idx >> 1)) & 15) << 1) + t
        return {"img": (core << 6) + (chip << 1) + half, "tok": t ^ (j >> 4)}

    def image_dev(j):
        return {"img": (core << 6) + (((j + idx) & 31) << 1) + half, "tok": idx & 1}

    z = img >> 4
    spot = (img & 8) + (core << 2) + ((img >> 1) & 3)
    mine = (t << 4) + spot

    def near(p):
        there = (z << 4) + (p & 8) + ((p & 3) << 1) + ((p >> 2) & 1)
        return {"img": there, "tok": p >> 4}

    def along_z(v):
        return {"img": (img & 15) + (v << 4), "tok": t}

    loads = [
        pltpu.make_async_copy(src, dst, load_sem.at[i])
        for i, (src, dst) in enumerate((
            (router_h, router_v), (scale_h, scale_v), (tokens_h, tok), (gout_h, gout), (w1_h, w1), (w2_h, w2)
        ))
    ]
    for load in loads:
        load.start()

    barrier = pltpu.get_barrier_semaphore()

    def greet(dev):
        pl.semaphore_signal(barrier, inc=1, device_id=dev, device_id_type=MESH)

    def greet_all(j, c):
        greet(image_dev(j))
        return c

    greet(partner)
    greet(sib)
    lax.fori_loop(1, 32, greet_all, 0)

    @pl.when(jnp.logical_not(selfish))
    def _():
        greet(image_dev(0))

    row = lax.broadcasted_iota(jnp.int32, (128, 1), 0)
    q, side, u, v = ((row >> 3) + (idx >> 1)) & 15, (row >> 2) & 1, (row >> 1) & 1, row & 1
    pack_out[...] = pick(side * 64 + (u ^ core) * C + 2 * q + v, 128)
    w, side, q, u = row >> 6, (row >> 5) & 1, (row >> 1) & 15, row & 1
    at = lax.broadcasted_iota(jnp.int32, (128, 256), 1)
    here = (at & 247) == q * 16 + side * 4 + u * 2 + (core ^ w)
    unpack_back[...] = jnp.where(here, 1.0, 0.0).astype(BF16)
    row = lax.broadcasted_iota(jnp.int32, (256, 1), 0)
    m_of, side, u, v = ((row >> 3) + idx) & 31, (row >> 2) & 1, (row >> 1) & 1, row & 1
    pack_back[...] = pick(side * 128 + (u ^ core) * E + 2 * m_of + v, 256)
    w, side, m_of, u = row >> 7, (row >> 6) & 1, (row >> 1) & 31, row & 1
    unpack_out[...] = pick(m_of * 8 + side * 4 + u * 2 + (core ^ w), 256)

    pairs = []

    def send(src, dst, dev):
        n = len(pairs)
        c = pltpu.make_async_remote_copy(
            src_ref=src, dst_ref=dst, send_sem=pair_ss.at[n], recv_sem=pair_rs.at[n],
            device_id=dev, device_id_type=MESH,
        )
        c.start()
        pairs.append(c)
        return c

    def quarters(own, other):
        return jnp.concatenate([own[:, :HALF], other[:, :HALF], own[:, HALF:], other[:, HALF:]], 0)

    def post(way, first, dev, slot):
        def one(m, c):
            pltpu.make_async_remote_copy(
                src_ref=msg_tx.at[way, m], dst_ref=msg_rx.at[way, slot],
                send_sem=a2a_ss.at[way], recv_sem=a2a_rs.at[way],
                device_id=dev(m), device_id_type=MESH,
            ).start()
            return c

        lax.fori_loop(max(first, 1), first + 16, one, 0)
        if first == 0:
            @pl.when(selfish)
            def _():
                pltpu.make_async_copy(msg_tx.at[way, 0], msg_rx.at[way, slot], a2a_rs.at[way]).start()

            @pl.when(jnp.logical_not(selfish))
            def _():
                one(0, 0)

    def to_experts(way, own, other):
        block = mm(pack_out[...], quarters(own, other)).astype(BF16).reshape(16, 8, HALF)
        msg_tx[way, 0:16] = block
        msg_tx[way, 16:32] = block
        post(way, 0, expert_dev, idx)
        post(way, 16, expert_dev, idx)

    def to_images(way, own, other):
        rows = quarters(own, other)
        for q in range(2):
            block = mm(pack_back[q * 128:q * 128 + 128, :], rows).astype(BF16)
            msg_tx[way, q * 16:q * 16 + 16] = block.reshape(16, 8, HALF)
            post(way, q * 16, image_dev, (idx & 30) + t)

    def landed(way):
        pltpu.make_async_copy(msg_rx.at[way], msg_rx.at[way], a2a_rs.at[way]).wait()

    def left_tx(way):
        @pl.when(selfish)
        def _():
            sent = msg_tx.at[way, pl.ds(0, 31)]
            pltpu.make_async_copy(sent, sent, a2a_ss.at[way]).wait()

        @pl.when(jnp.logical_not(selfish))
        def _():
            pltpu.make_async_copy(msg_tx.at[way], msg_tx.at[way], a2a_ss.at[way]).wait()

    def gather(way, w):
        order = (unpack_out if way < 2 else unpack_back)
        n = order.shape[0] // 2
        out = mm(order[w * n:w * n + n, :], msg_rx[way].reshape(256, HALF))
        return out[0:n // 2], out[n // 2:]

    loads[0].wait()
    loads[1].wait()
    row = lax.broadcasted_iota(jnp.int32, (E, 1), 0)
    expert = ((row & 31) >> 1) * 4 + ((row >> 5) ^ t) * 2 + (row & 1)
    router_b = mm(pick(expert, E), router_v[...]).astype(BF16)
    router_t = router_b.astype(F32)
    at = lax.broadcasted_iota(jnp.int32, (E, E), 1)
    scale = jnp.sum(jnp.where(at == expert, scale_v[...], 0.0), 1, keepdims=True)
    column = lax.rsqrt(jnp.sum(router_t * router_t, 1, keepdims=True) + EPSILON) * scale
    loads[2].wait()
    tok_f = tok[...].astype(F32)
    inv_x = to_row(lax.rsqrt(jnp.sum(tok_f * tok_f, 1, keepdims=True) + EPSILON))
    logit = mm_nt(router_b, tok[...]) * inv_x * column
    expo = jnp.exp(logit)
    den_part = jnp.sum(expo, 1, keepdims=True)
    den_row = to_row(den_part)
    den_tx[...] = jnp.broadcast_to(jnp.concatenate([den_row, den_row], 1), (8, 128))
    pw = expo.astype(BF16)
    numer = mm(pw, tok[...])
    part_tx[0:C, :] = numer[C:].astype(BF16)

    pl.semaphore_wait(barrier, 33 + jnp.where(selfish, 0, 1))

    c_den = send(den_tx, den_rx, partner)
    c_num = send(part_tx.at[0:C], part_rx.at[0:C], partner)
    row_sum = jnp.sum(expo, 0, keepdims=True)
    comb = expo / row_sum
    comb_b = comb.astype(BF16)
    loads[3].wait()
    dys = mm(comb_b, gout[...])
    part_tx[C:, :] = dys[C:].astype(BF16)
    c_dys = send(part_tx.at[C:], part_rx.at[C:], partner)
    info_tx[0:C, :] = logit[C:]
    info_tx[C:C + 8, :] = jnp.broadcast_to(inv_x, (8, M))
    info_tx[C + 8:, :] = jnp.broadcast_to(row_sum, (8, M))
    c_info = send(info_tx, info_rx, partner)
    c_gout = send(gout, gout_all.at[M:], partner)
    c_den.wait_recv()
    den = den_part[0:C] + to_col(den_rx[0:1, 0:E])[C:]
    c_num.wait_recv()
    own_a[0:C, :] = ((numer[0:C] + part_rx[0:C, :].astype(F32)) / den).astype(BF16)
    c_s1 = send(own_a.at[0:C], sib_a.at[0:C], sib)
    c_s1.wait_recv()
    to_experts(0, own_a[0:C, :], sib_a[0:C, :])
    c_dys.wait_recv()
    own_a[C:, :] = (dys[0:C] + part_rx[C:, :].astype(F32)).astype(BF16)
    c_s2 = send(own_a.at[C:], sib_a.at[C:], sib)
    c_s2.wait_recv()
    to_experts(1, own_a[C:, :], sib_a[C:, :])
    c_tok = send(tok, tok_all.at[M:], partner)

    def arrive(way, rows):
        lo = (way % 2) * E
        landed(way)
        left, right = gather(way, 1)
        swap_tx[lo:lo + E, :HALF] = left.astype(BF16)
        swap_tx[lo:lo + E, HALF:] = right.astype(BF16)
        c = send(swap_tx.at[lo:lo + E], rows.at[E:], sib)
        left, right = gather(way, 0)
        rows[0:E, :HALF] = left.astype(BF16)
        rows[0:E, HALF:] = right.astype(BF16)
        c.wait_recv()

    arrive(0, x_v)
    loads[4].wait()
    loads[5].wait()

    def expert_in(n, c):
        at = pl.ds(pl.multiple_of(n * 256, 256), 256)
        act = mm(x_v[...], w1[:, at])
        phi = 0.5 * (1.0 + lax.erf(act * ROOT_HALF))
        hid[:, at] = (act * phi).astype(BF16)
        slope[:, at] = phi + act * jnp.exp(-0.5 * act * act) * DENSITY
        return c

    lax.fori_loop(0, H // 256, expert_in, 0, unroll=True)

    def expert_out(n, c):
        at = pl.ds(pl.multiple_of(n * 256, 256), 256)
        part = mm(hid[...], w2[:, at]).astype(BF16)
        own_b[0:E, at] = part[0:E]
        swap2_tx[0:E, at] = part[E:]
        return c

    lax.fori_loop(0, D // 256, expert_out, 0, unroll=True)
    c_w2 = send(swap2_tx.at[0:E], swap2_rx.at[0:E], sib)
    c_w2.wait_recv()
    to_images(2, own_b[0:E, :], swap2_rx[0:E, :])
    arrive(1, z_v)

    def expert_back(n, c):
        at = pl.ds(pl.multiple_of(n * 256, 256), 256)
        dh = mm_nt(z_v[...], w2[at, :])
        dact[:, at] = (dh * slope[:, at]).astype(BF16)
        return c

    lax.fori_loop(0, H // 256, expert_back, 0, unroll=True)

    def expert_back_in(n, c):
        at = pl.ds(pl.multiple_of(n * 256, 256), 256)
        part = mm_nt(dact[...], w1[at, :]).astype(BF16)
        own_b[E:, at] = part[0:E]
        swap2_tx[E:, at] = part[E:]
        return c

    lax.fori_loop(0, D // 256, expert_back_in, 0, unroll=True)
    c_w3 = send(swap2_tx.at[E:], swap2_rx.at[E:], sib)
    c_w3.wait_recv()
    to_images(3, own_b[E:, :], swap2_rx[E:, :])

    def returned(way):
        lo = (way % 2) * C
        landed(way)
        left, right = gather(way, 1)
        swap3_tx[lo:lo + C, :HALF] = left.astype(BF16)
        swap3_tx[lo:lo + C, HALF:] = right.astype(BF16)
        c = send(swap3_tx.at[lo:lo + C], swap3_rx.at[lo:lo + C], sib)
        left, right = gather(way, 0)
        c.wait_recv()
        return (jnp.concatenate([left, right], 1) + swap3_rx[lo:lo + C, :].astype(F32)).astype(BF16)

    ys_v[0:C, :] = returned(2)
    c_info.wait_recv()
    logit_o, inv_o, sum_o = info_rx[0:C, :], info_rx[C:C + 1, :], info_rx[C + 8:C + 9, :]
    expo_o = jnp.exp(logit_o)
    comb_m, comb_o = comb[0:C], expo_o / sum_o
    c_gout.wait_recv()
    share, share_o = expo[0:C] / den, expo_o / den
    factor, factor_o = column[0:C] * inv_x, column[0:C] * inv_o
    ys = ys_v[0:C, :]
    dcomb, dcomb_o = mm_nt(ys, gout[...]), mm_nt(ys, gout_all[M:, :])
    row_own = jnp.sum(comb_m * dcomb, 0, keepdims=True)
    row_o = jnp.sum(comb_o * dcomb_o, 0, keepdims=True)
    row_tx[0:8, :] = jnp.broadcast_to(row_o, (8, M))
    row_tx[8:, :] = jnp.broadcast_to(row_own, (8, M))
    c_row = send(row_tx, row_rx, partner)
    c_ys = send(ys_v.at[0:C], ys_v.at[C:], partner)
    c_tok.wait_recv()
    dxs = returned(3)
    c_row.wait_recv()
    dlc = comb_m * (dcomb - row_own - row_rx[0:1, :])
    dlc_o = comb_o * (dcomb_o - row_o - row_rx[8:9, :])
    ddisp, ddisp_o = mm_nt(dxs, tok[...]), mm_nt(dxs, tok_all[M:, :])
    corr = jnp.sum(share * ddisp, 1, keepdims=True) + jnp.sum(share_o * ddisp_o, 1, keepdims=True)
    grad_l = share * (ddisp - corr) + dlc
    grad_o = share_o * (ddisp_o - corr) + dlc_o
    grad_q, grad_qo = (grad_l * factor).astype(BF16), (grad_o * factor_o).astype(BF16)
    outer = mm(jnp.concatenate([grad_q, grad_qo], 1), tok_all[...])
    wide = jnp.concatenate([outer, jnp.zeros((C, 4 * PIECE - D), F32)], 1).astype(BF16)
    for p in range(16):
        r, q = p // 4, p % 4
        ar_tx[p] = wide[8 * r:8 * r + 8, PIECE * q:PIECE * q + PIECE]

    def scatter(j, c):
        p = (spot + j) & 15
        pltpu.make_async_remote_copy(
            src_ref=ar_tx.at[p], dst_ref=ar_rx1.at[spot], send_sem=ar_ss.at[0], recv_sem=ar_rs.at[0],
            device_id=near((t << 4) + p), device_id_type=MESH,
        ).start()
        return c

    lax.fori_loop(1, 16, scatter, 0)
    ar_rx1[spot] = ar_tx[spot]

    gd_v[0:C, :] = (dxs.astype(F32) / den).astype(BF16)
    c_gd = send(gd_v.at[0:C], gd_v.at[C:], partner)
    gq_tx[...] = grad_qo
    c_gq = send(gq_tx, gq_rx, partner)
    sig_tx[...] = jnp.broadcast_to(jnp.sum(grad_o * logit_o, 0, keepdims=True), (8, M))
    c_sig = send(sig_tx, sig_rx, partner)
    signal = jnp.sum(grad_l * logit[0:C], 0, keepdims=True)
    c_ys.wait_recv()
    combined_ref[...] = mm_tn(comb_b, ys_v[...]).astype(BF16)

    def counted(ref, n, sem):
        pltpu.make_async_copy(ref.at[0:n], ref.at[0:n], sem).wait()

    def total_of(rx, n):
        acc = rx[0].astype(F32)
        for j in range(1, n):
            acc = acc + rx[j].astype(F32)
        return acc.astype(BF16)

    counted(ar_rx1, 15, ar_rs.at[0])
    ar_rx2[z] = total_of(ar_rx1, 16)
    for d in range(1, 8):
        pltpu.make_async_remote_copy(
            src_ref=ar_rx2.at[z], dst_ref=ar_rx2.at[z], send_sem=ar_ss.at[1], recv_sem=ar_rs.at[1],
            device_id=along_z((z + d) & 7), device_id_type=MESH,
        ).start()

    xt_ref[...] = x_v[...].T
    dact_ref[...] = dact[...]
    counted(ar_rx2, 7, ar_rs.at[1])
    ar_rx3[mine] = total_of(ar_rx2, 8)

    def collect(j, c):
        pltpu.make_async_remote_copy(
            src_ref=ar_rx3.at[mine], dst_ref=ar_rx3.at[mine], send_sem=ar_ss.at[2], recv_sem=ar_rs.at[2],
            device_id=near((mine + j) & 31), device_id_type=MESH,
        ).start()
        return c

    lax.fori_loop(1, 32, collect, 0)
    ht_ref[...] = hid[...].T
    z_ref[...] = z_v[...]
    router_f = router_v[...].astype(F32)
    inv_p = lax.rsqrt(jnp.sum(router_f * router_f, 1, keepdims=True) + EPSILON)
    c_gd.wait_recv()
    c_gq.wait_recv()
    c_sig.wait_recv()
    coef = to_col(inv_x * inv_x * (signal + sig_rx[0:1, :]))
    weights = jnp.concatenate([pw, grad_q, gq_rx[...]], 0)
    values = jnp.concatenate([gd_v[...], router_b], 0)
    gtok_ref[...] = (mm_tn(weights, values) - coef * tok[...].astype(F32)).astype(BF16)
    for way in range(4):
        left_tx(way)
    for c in pairs:
        c.wait_send()
    counted(ar_tx, 15, ar_ss.at[0])
    counted(ar_rx2, 7, ar_ss.at[1])
    counted(ar_rx3, 31, ar_rs.at[2])
    counted(ar_rx3, 31, ar_ss.at[2])
    whole = jnp.concatenate(
        [jnp.concatenate([ar_rx3[4 * r + q] for q in range(4)], 1)[:, :D] for r in range(8)], 0
    )
    row = lax.broadcasted_iota(jnp.int32, (E, 1), 0)
    whole = mm(pick(((row >> 1) & 1) * C + (row >> 2) * 2 + (row & 1), E), whole)
    total = jnp.sum(whole * router_f, 1, keepdims=True)
    groute_ref[...] = whole - inv_p * inv_p * total * router_f
    gscale_ref[...] = to_row(total) / scale_v[...]


def finish(
    combined_v, gtok_v, groute_v, gscale_v, xt_ref, z_ref, ht_ref, dact_ref,
    combined_h, gtok_h, groute_h, gscale_h, g1_h, g2_h, g1, g2, sem,
):
    copies = []

    def out(src, dst):
        c = pltpu.make_async_copy(src, dst, sem.at[len(copies)])
        c.start()
        copies.append(c)

    def product(left, right, g, g_h, n):
        for i in range(n):
            at = pl.ds(i * 256, 256)
            g[at, :] = mm(left[at, :], right[...]).astype(BF16)
            out(g.at[at], g_h.at[at])

    out(combined_v, combined_h)
    out(gtok_v, gtok_h)
    out(groute_v, groute_h)
    out(gscale_v, gscale_h)
    product(xt_ref, dact_ref, g1, g1_h, 5)
    product(ht_ref, z_ref, g2, g2_h, 4)
    for c in copies:
        c.wait()


def shards(tokens, grad_out, router, slot_scale, w_in, w_out):
    hbm = pl.BlockSpec(memory_space=pltpu.HBM)
    vmem = pl.BlockSpec(memory_space=pltpu.VMEM)
    rows = pltpu.VMEM((128, D), BF16)
    few = pltpu.VMEM((E, D), BF16)
    tile = pltpu.VMEM((8, 128), F32)
    half_rows = pltpu.VMEM((128, H), BF16)
    msgs = pltpu.VMEM((4, 32, 8, HALF), BF16)
    dma = pltpu.SemaphoreType.DMA
    shapes = [
        jax.ShapeDtypeStruct((M, D), BF16),
        jax.ShapeDtypeStruct((M, D), BF16),
        jax.ShapeDtypeStruct((E, D), F32),
        jax.ShapeDtypeStruct((1, E), F32),
    ]
    factors = [
        jax.ShapeDtypeStruct((D, 128), BF16),
        jax.ShapeDtypeStruct((128, D), BF16),
        jax.ShapeDtypeStruct((H, 128), BF16),
        jax.ShapeDtypeStruct((128, H), BF16),
    ]
    grads = [jax.ShapeDtypeStruct((D, H), BF16), jax.ShapeDtypeStruct((H, D), BF16)]
    out = pl.pallas_call(
        layer,
        out_shape=shapes + factors,
        in_specs=[hbm] * 6,
        out_specs=[vmem] * 8,
        scratch_shapes=[
            pltpu.VMEM((2 * M, D), BF16), pltpu.VMEM((2 * M, D), BF16), pltpu.VMEM((D, H), BF16), pltpu.VMEM((H, D), BF16),
            pltpu.VMEM((E, D), BF16), pltpu.VMEM((1, E), F32),
            pltpu.VMEM((128, 128), BF16), pltpu.VMEM((256, 256), BF16),
            pltpu.VMEM((256, 256), BF16), pltpu.VMEM((128, 256), BF16),
            few, few, tile, tile, pltpu.VMEM((48, M), F32), pltpu.VMEM((48, M), F32),
            few, few, msgs, msgs, rows, rows, rows,
            half_rows, half_rows, pltpu.VMEM((128, H), F32), rows, rows, rows, few, few, few,
            pltpu.VMEM((16, M), F32), pltpu.VMEM((16, M), F32),
            few, pltpu.VMEM((C, M), BF16), pltpu.VMEM((C, M), BF16), tile, tile,
            pltpu.VMEM((16, 8, PIECE), BF16), pltpu.VMEM((16, 8, PIECE), BF16),
            pltpu.VMEM((8, 8, PIECE), BF16), pltpu.VMEM((32, 8, PIECE), BF16),
            dma((6,)), dma((19,)), dma((19,)), dma((4,)), dma((4,)), dma((3,)), dma((3,)),
        ],
        name="layer",
        compiler_params=pltpu.CompilerParams(
            collective_id=0, has_side_effects=True, vmem_limit_bytes=int(LIMIT * 2**20)
        ),
    )(*[
        pltpu.with_memory_space_constraint(x, pltpu.HBM)
        for x in (tokens[0], grad_out[0], w_in[0], w_out[0], router.T, slot_scale[None, :])
    ])
    combined, grad_tokens, grad_route, grad_scale, grad_w_in, grad_w_out = pl.pallas_call(
        finish,
        out_shape=shapes + grads,
        in_specs=[vmem] * 8,
        out_specs=[hbm] * 6,
        scratch_shapes=[pltpu.VMEM((D, H), BF16), pltpu.VMEM((H, D), BF16), dma((13,))],
        name="finish",
        compiler_params=pltpu.CompilerParams(vmem_limit_bytes=20 * 2**20),
    )(*out)
    return (
        combined[None],
        grad_tokens[None],
        grad_route.T,
        grad_scale[0],
        grad_w_in[None],
        grad_w_out[None],
    )


def solution(mesh):
    return jax.shard_map(
        shards,
        mesh=mesh,
        in_specs=(
            P("img", "tok", None),
            P("img", "tok", None),
            P(),
            P(),
            P("img", None, "tok"),
            P("img", "tok", None),
        ),
        out_specs=(
            P("img", "tok", None),
            P("img", "tok", None),
            P(),
            P(),
            P("img", None, "tok"),
            P("img", "tok", None),
        ),
        check_vma=False,
    )
```
